1024 devices in a mesh: dp: 16 (over x, y), expert: 64 (over z, core).
Axes of the slice: x: 4, y: 4, z: 32, core: 2. Of those that a mesh axis runs over, the one named last changes fastest.
Arguments:
- hidden: bfloat16 [2048, 16384], P('dp', 'expert'), may hold values from -6 to 6
- expert_ids: int32 [2048, 8], P(('dp', 'expert')), may hold values from 0 to 15, all different within a row; in each aligned block of 2 rows (0 to 1, 2 to 3, ...) at most 2 rows name the same one
- route_weight: float32 [2048, 8], P(('dp', 'expert')), may hold values from 0.1 to 1
- cotangent: bfloat16 [2048, 7168], P(('dp', 'expert')), may hold values from -6 to 6
- w_down: bfloat16 [16384, 7168], P('expert'), may hold values from -0.1875 to 0.1875
Outputs:
- mixed: bfloat16 [2048, 7168], P(('dp', 'expert'))
- grad_hidden: bfloat16 [2048, 16384], P('dp', 'expert')
- grad_down: bfloat16 [16384, 7168], P('expert', 'dp')
The draws below stay inside these ranges and needn't reach their ends.
Inputs may be any that keep to these rules, and one draw needn't show every extreme that they name: `expert_ids`: each row names 8 different experts. In each aligned block of 2 rows (the tokens of one device) no expert is named more than 2 times, a bound that some block reaches.
All inputs are finite; a program needn't handle non-finite values.
Results may differ from the reference program's by a relative error of at most 0.018.
Values may be sent and summed in bfloat16 or wider, within the bound.
A program may use at most 32 MiB of HBM per device.

```python
import math
import jax
import jax.numpy as jnp
import numpy as np
from jax import lax

D = 7168
FF = 1024
TOK_DEV = 2
EXPERTS = 16
TOP = 8
CAP = 2
FF_DEV = 256
SLOTS = 128
TOKENS = 2048
N_DP = 16


def block_scale(own_key, dims, cuts, least, largest):
    gain, own = 1.0, jax.random.fold_in(own_key, 6)
    for axis_at, blocks in cuts:
        heights = jnp.exp(jax.random.uniform(jax.random.fold_in(own, axis_at), (blocks,), jnp.float32, least / len(cuts), largest / len(cuts)))
        gain = gain * jnp.repeat(heights, dims[axis_at] // blocks).reshape([-1 if axis == axis_at else 1 for axis in range(len(dims))])
    return gain


def deal_out(own_key, own, number, rows, amount, top, bound, lean):
    sequence = jax.random.permutation(own_key, amount)
    packed, common = load_shares(amount, rows * top, bound, lean, True), load_shares(amount, rows * top, bound, lean, False)
    places = jnp.arange(amount)

    def named(lengths, turn):
        used = int((lengths > 0).sum())
        fixed = max(1, used // 4)
        shifted = fixed + (places - fixed + turn * (used - fixed)) % max(1, amount - fixed)
        return jnp.zeros((amount,), jnp.int32).at[sequence[jnp.where(places < fixed, places, shifted)]].set(jnp.asarray(lengths, jnp.int32))

    lengths = jnp.where(number % 4 == 0, named(packed, number // 4), named(common, number - number // 4 - 1))
    mixed = jax.random.permutation(jax.random.fold_in(own, 3), amount)
    source_of, receiver = mixed[0:amount // 2 * 2:2], mixed[1:amount // 2 * 2:2]
    slack = jnp.minimum(lengths[source_of] - 1, bound - lengths[receiver]) // 2
    slack = jnp.where((source_of == sequence[0]) | (receiver == sequence[0]) | (lengths[receiver] == 0), 0, jnp.maximum(slack, 0))
    shifted = jax.random.randint(jax.random.fold_in(own, 4), (amount // 2,), 0, 1 << 20) % (slack + 1)
    lengths = lengths.at[source_of].add(-shifted).at[receiver].add(shifted)
    members = jnp.searchsorted(jnp.cumsum(lengths), jnp.arange(rows * top), side="right").astype(jnp.int32)
    grid = members.reshape(top, rows).T
    grid = grid[jax.random.permutation(jax.random.fold_in(own, 1), rows)]
    turn = jax.random.randint(jax.random.fold_in(own, 2), (rows, 1), 0, top)
    return jnp.take_along_axis(grid, (jnp.arange(top)[None, :] + turn) % top, axis=1)


def load_shares(count, total, reach, slope, full):
    portions = [(1 << 20) // math.isqrt(rank ** slope) + 1 for rank in range(1, count + 1)]
    largest = reach if full else min(reach, max(-(-total // count), total * portions[0] // sum(portions)))
    least = 1 if total - largest >= count - 1 else 0
    counts, spare = [largest] + [least] * (count - 1), total - largest - least * (count - 1)
    while spare > 0:
        movable = [i for i in range(1, count) if counts[i] < largest] or [i for i in range(1, count) if counts[i] < reach]
        whole, budget = sum([portions[i] for i in movable]), spare
        for i in movable:
            more = min(reach - counts[i], max(1, budget * portions[i] // whole), spare)
            counts[i] = counts[i] + more
            spare = spare - more
    return np.array(counts)


def gaussian(own_key, dims, scale, bound, pieces=(), kind=jnp.bfloat16):
    values = jax.random.normal(own_key, dims, jnp.float32) * scale
    if len(pieces) > 0:
        values = block_scale(own_key, dims, pieces, -0.22, 0.18) * values
    return jnp.clip(values, min=-bound, max=bound).astype(kind)


def setup_inputs(seed: int = 0) -> dict:
    seeds = jax.random.split(jax.random.key(seed), 6)
    hidden = gaussian(seeds[0], (N_DP * SLOTS, EXPERTS * FF), 1.0, 6.0, ((0, 16), (1, 64)))
    expert_ids_keys = jax.random.split(jax.random.fold_in(seeds[1], 1), TOKENS // TOK_DEV)
    expert_ids_turns = jax.random.permutation(jax.random.fold_in(seeds[1], 3), TOKENS // TOK_DEV)
    expert_ids = jax.vmap(lambda own, number: deal_out(jax.random.fold_in(seeds[1], 2), own, number, TOK_DEV, EXPERTS, TOP, CAP, 2))(expert_ids_keys, expert_ids_turns).reshape((TOKENS, TOP))
    route_weight = jnp.clip(jnp.exp(math.log(1.0) - 2.3025851 * jax.random.uniform(seeds[2], (TOKENS, TOP), jnp.float32) ** block_scale(seeds[2], (TOKENS, TOP), ((0, 1024),), -0.2, 0.2)), 0.1, 1.0)
    cotangent = gaussian(seeds[3], (TOKENS, D), 1.0, 6.0, ((0, 1024),))
    w_down = gaussian(seeds[4], (EXPERTS * FF, D), FF ** -0.5, 0.1875, ((0, 64),))
    return {"hidden": hidden, "expert_ids": expert_ids, "route_weight": route_weight, "cotangent": cotangent, "w_down": w_down}


def reference(hidden, expert_ids, route_weight, cotangent, w_down):
    blocks = TOKENS // TOK_DEV
    routed = TOK_DEV * TOP
    slot_all = blocks * CAP
    chosen = expert_ids.reshape(blocks, routed).astype(jnp.int32)
    onehot = (chosen[:, :, None] == jnp.arange(EXPERTS, dtype=jnp.int32)[None, None, :]).astype(jnp.int32)
    position = jnp.sum(jnp.cumsum(onehot, axis=1) * onehot, axis=2) - 1
    slot_row = (jnp.arange(blocks, dtype=jnp.int32)[:, None] * CAP + position).astype(jnp.int32)
    target_slot = (chosen * slot_all + slot_row).reshape(-1).astype(jnp.int32)
    source_index = jnp.arange(TOKENS * TOP, dtype=jnp.int32)
    slot_table = jnp.zeros((EXPERTS * slot_all,), jnp.int32).at[target_slot].set(source_index)
    live_mask = jnp.zeros((EXPERTS * slot_all,), jnp.float32).at[target_slot].set(1.0)
    slot_table = slot_table.reshape(EXPERTS, slot_all)
    live_mask = live_mask.reshape(EXPERTS, slot_all)
    token_table = (slot_table // TOP).astype(jnp.int32)
    weight_table = route_weight.reshape(-1)[slot_table] * live_mask
    hidden_by_expert = hidden.reshape(slot_all, EXPERTS, FF).transpose(1, 0, 2)
    down_by_expert = w_down.reshape(EXPERTS, FF, D)

    def per_group(running, operands):
        hidden_group, grad_group = operands
        quarter_sum = lax.dot_general(hidden_group, grad_group, (((0,), (0,)), ((), ())),
                                      preferred_element_type=jnp.float32).astype(jnp.bfloat16)
        return running + quarter_sum.astype(jnp.float32), None

    def per_expert(mixed_sum, operands):
        hidden_rows, down_rows, token_index, row_weights = operands
        summed_parts = jnp.zeros((slot_all, D), jnp.float32)
        for quarter in range(4):
            first_unit = quarter * FF_DEV
            quarter_out = jnp.dot(hidden_rows[:, first_unit:first_unit + FF_DEV],
                                  down_rows[first_unit:first_unit + FF_DEV],
                                  preferred_element_type=jnp.float32).astype(jnp.bfloat16)
            summed_parts = summed_parts + quarter_out.astype(jnp.float32)
        mixed_sum = mixed_sum.at[token_index].add(row_weights[:, None] * summed_parts)
        grad_rows = (row_weights[:, None] * cotangent[token_index].astype(jnp.float32)).astype(jnp.bfloat16)
        grad_part = lax.dot_general(grad_rows, down_rows, (((1,), (1,)), ((), ())),
                                    preferred_element_type=jnp.float32).astype(jnp.bfloat16)
        running, _ = lax.scan(per_group, jnp.zeros((FF, D), jnp.float32),
                              (hidden_rows.reshape(N_DP, SLOTS, FF), grad_rows.reshape(N_DP, SLOTS, D)))
        return mixed_sum, (grad_part, running.astype(jnp.bfloat16))

    mixed_sum, outputs = lax.scan(per_expert, jnp.zeros((TOKENS, D), jnp.float32),
                                  (hidden_by_expert, down_by_expert, token_table, weight_table))
    grad_parts, down_grads = outputs
    mixed = mixed_sum.astype(jnp.bfloat16)
    grad_hidden = grad_parts.transpose(1, 0, 2).reshape(slot_all, EXPERTS * FF)
    grad_down = down_grads.reshape(EXPERTS * FF, D)
    return (mixed, grad_hidden, grad_down)
```

```python
import jax
import jax.numpy as jnp
from jax import lax
from jax.sharding import PartitionSpec as P


def body(hidden, expert_ids, route_weight, cotangent, w_down):
    tok_dev, width = cotangent.shape
    devices = lax.axis_size("expert")
    experts = devices // 4
    mine = lax.axis_index("expert") // 4
    onehot = (expert_ids[:, :, None] == jnp.arange(experts, dtype=jnp.int32)).astype(jnp.float32)
    named = jnp.sum(onehot, axis=1)
    weight = jnp.sum(onehot * route_weight[:, :, None], axis=1)
    table = lax.all_gather(jnp.concatenate([named, weight], axis=1), "expert", axis=0, tiled=True)
    rows = lax.all_gather(cotangent, "expert", axis=0, tiled=True)
    n_all = lax.dynamic_index_in_dim(table, mine, axis=1, keepdims=False).reshape(devices, 2)
    w_all = lax.dynamic_index_in_dim(table, mine + experts, axis=1, keepdims=False).reshape(devices, 2)
    n0, n1, w0, w1 = n_all[:, 0:1], n_all[:, 1:2], w_all[:, 0:1], w_all[:, 1:2]
    pairs = hidden.astype(jnp.float32).reshape(devices, 2, -1)
    h0, h1 = pairs[:, 0], pairs[:, 1]
    hw = jnp.stack([w0 * h0, w1 * jnp.where(n0 > 0, h1, h0)], axis=1)
    hw = hw.reshape(2 * devices, -1).astype(jnp.bfloat16)
    out = jnp.dot(hw, w_down, preferred_element_type=jnp.float32).astype(jnp.bfloat16)
    mixed = lax.psum_scatter(out, "expert", scatter_dimension=0, tiled=True)
    term = lax.dot_general(hw, rows, (((0,), (0,)), ((), ())), preferred_element_type=jnp.float32)
    grad_down = lax.psum_scatter(term.astype(jnp.bfloat16), "dp", scatter_dimension=1, tiled=True)
    back = lax.dot_general(rows, w_down, (((1,), (1,)), ((), ())), preferred_element_type=jnp.float32)
    back = back.reshape(devices, 2, -1)
    g0, g1 = w0 * back[:, 0], w1 * back[:, 1]
    first = jnp.where(n0 > 0, g0, g1)
    second = jnp.where(n0 * n1 > 0, g1, 0.0)
    grad_hidden = jnp.stack([first, second], axis=1).reshape(2 * devices, -1).astype(jnp.bfloat16)
    return (mixed, grad_hidden, grad_down)


def solution(mesh):
    return jax.shard_map(
        body,
        mesh=mesh,
        in_specs=(
            P("dp", "expert"),
            P(("dp", "expert"), None),
            P(("dp", "expert"), None),
            P(("dp", "expert"), None),
            P("expert", None),
        ),
        out_specs=(P(("dp", "expert"), None), P("dp", "expert"), P("expert", "dp")),
        check_vma=False,
    )
```

```python
import functools

import jax
import jax.numpy as jnp
from jax import lax
from jax.experimental import pallas as pl
from jax.experimental.pallas import tpu as pltpu
from jax.sharding import PartitionSpec as P

MESH = pl.DeviceIdType.MESH
F32, BF16 = jnp.float32, jnp.bfloat16
NT = (((1,), (1,)), ((), ()))
TN = (((0,), (0,)), ((), ()))
LAG = 4


def onehot(rows, columns, dtype):
    return (rows == columns).astype(F32).astype(dtype)


def kernel(nd, ne, radix, tok_ref, hid_ref, tab_ref, w_ref, mixed_ref, gh_ref, gd_ref,
           w2, sib_tok, merge, sib_hid, table, flat, ring, y_buf, rs_in, rs_out, fin, mix_in,
           hw_t, blocks, g_acc, gh_send, gh_in, acc, acc_in,
           local_sem, sib_s, sib_r, r1_s, r1_r, r2_s, r2_r, ag_s, ag_r, rs_s, rs_r,
           hw_s, hw_r, bl_s, bl_r):
    nz, half = ne // 2, ne // 4
    toks = 4 * half
    units = hid_ref.shape[1]
    tiles = w2.shape[2] // 128
    d, p = lax.axis_index("dp"), lax.axis_index("expert")
    z, c = p // 2, lax.rem(p, 2)
    way = 1 - 2 * c
    expert = p // 4
    base = 1 - c
    sibling = (d, p + 1 - 2 * c)
    ahead = (d, lax.rem(z + way + nz, nz) * 2 + c)
    behind = (d, lax.rem(z - way + nz, nz) * 2 + c)
    groups = ne // radix
    group, member = p // radix, lax.rem(p, radix)

    def copy(src, dst, send, recv, to):
        return pltpu.make_async_remote_copy(src_ref=src, dst_ref=dst, send_sem=send, recv_sem=recv,
                                            device_id=to, device_id_type=MESH)

    w_own = pltpu.make_async_copy(w_ref, w2.at[0], local_sem.at[0])
    w_own.start()

    barrier = pltpu.get_barrier_semaphore()
    for to in (sibling, ahead, behind):
        pl.semaphore_signal(barrier, inc=1, device_id=to, device_id_type=MESH)

    def greet_member(i, _):
        to = (d, group * radix + lax.rem(member + i, radix))
        pl.semaphore_signal(barrier, inc=1, device_id=to, device_id_type=MESH)
        return 0

    def greet_group(i, _):
        to = (d, lax.rem(p + i * radix, ne))
        pl.semaphore_signal(barrier, inc=1, device_id=to, device_id_type=MESH)
        return 0

    def greet_dp(i, _):
        pl.semaphore_signal(barrier, inc=1, device_id=(lax.rem(d + i, nd), p), device_id_type=MESH)
        return 0

    lax.fori_loop(1, radix, greet_member, 0)
    lax.fori_loop(1, groups, greet_group, 0)
    lax.fori_loop(1, nd, greet_dp, 0)
    table[p] = tab_ref[...]
    merge[:, pl.ds(pl.multiple_of(8 * c, 8), 8), :] = tok_ref[...].astype(F32).reshape(nd, 8, 128)
    pl.semaphore_wait(barrier, 3 + (radix - 1) + (groups - 1) + (nd - 1))

    tok_copy = copy(tok_ref, sib_tok, sib_s.at[0], sib_r.at[0], sibling)
    hid_copy = copy(hid_ref, sib_hid, sib_s.at[1], sib_r.at[1], sibling)
    w_copy = copy(w_ref, w2.at[1], sib_s.at[2], sib_r.at[2], sibling)
    tok_copy.start()

    def one(i, back):
        to = lax.rem(member + i, radix)
        slot = group * radix + lax.rem(member + radix - i, radix) if back else p
        return copy(table.at[p], table.at[slot], r1_s.at[i], r1_r.at[i], (d, group * radix + to))

    def two(i, back):
        to = lax.rem(p + i * radix, ne)
        slot = lax.rem(group + groups - i, groups) if back else group
        return copy(table.at[pl.ds(group * radix, radix)], table.at[pl.ds(slot * radix, radix)],
                    r2_s.at[i], r2_r.at[i], (d, to))

    def each(low, high, step):
        def run(i, _):
            step(i)
            return 0
        lax.fori_loop(low, high, run, 0)

    each(1, radix, lambda i: one(i, False).start())
    hid_copy.start()
    w_copy.start()

    def ag(t):
        return copy(ring.at[t], ring.at[t + 1], ag_s.at[t], ag_r.at[t], ahead)

    def rs(t):
        return copy(rs_out.at[t], rs_in.at[t + 1], rs_s.at[t], rs_r.at[t], behind)

    def ag_step(t):
        ag(t - 1).wait_recv()
        if isinstance(t, int) and t == half - 1:
            @pl.when(c == 0)
            def _():
                ag(t).start()
        else:
            ag(t).start()

    tok_copy.wait_recv()
    merge[:, pl.ds(pl.multiple_of(8 * (1 - c), 8), 8), :] = sib_tok[...].astype(F32).reshape(nd, 8, 128)
    ring[0] = merge[...].reshape(16 * nd, 128).astype(BF16)
    ag(0).start()

    each(1, radix, lambda i: one(i, True).wait_recv())
    each(1, groups, lambda i: two(i, False).start())
    done = 1
    if done < half:
        ag_step(done)
        done += 1
    each(1, groups, lambda i: two(i, True).wait_recv())
    hid_copy.wait_recv()

    def flatten(i):
        flat[pl.ds(2 * i, 2), :] = table[i]
    for i in range(ne):
        flatten(i)
    row = lax.broadcasted_iota(jnp.int32, (toks, 4 * nz), 0)
    column = lax.broadcasted_iota(jnp.int32, (toks, 4 * nz), 1)

    def place_of(token):
        chip = z - way * ((token >> 2) + base)
        chip = jnp.where(chip < 0, chip + nz, chip)
        chip = jnp.where(chip >= nz, chip - nz, chip)
        return chip * 4 + (token & 3)

    place = place_of(row)
    picked = jnp.dot(onehot(place, column, F32), flat[...], preferred_element_type=F32,
                     precision=lax.Precision.HIGHEST)
    lane = lax.broadcasted_iota(jnp.int32, (toks, 128), 1)

    def coefficient(k):
        return jnp.sum(jnp.where(lane == expert + 32 * k, picked, 0.0), axis=1, keepdims=True)

    keep, shift, give = coefficient(0), coefficient(1), coefficient(2)
    both = jnp.concatenate([hid_ref[...], sib_hid[...]], axis=1)
    at = jnp.dot(onehot(place, column, BF16), both, preferred_element_type=F32)
    before = jnp.dot(onehot(place - 1, column, BF16), both, preferred_element_type=F32)
    hw = (keep * at + shift * before).astype(BF16)
    spot_row = lax.broadcasted_iota(jnp.int32, (toks, 2 * toks), 0)
    spot_column = lax.broadcasted_iota(jnp.int32, (toks, 2 * toks), 1)
    turned = lax.dot_general(hw[:, :units], onehot(spot_row, spot_column, BF16), TN, preferred_element_type=F32)
    turned = turned + lax.dot_general(hw[:, units:], onehot(spot_row + toks, spot_column, BF16), TN,
                                      preferred_element_type=F32)
    hw_t[d] = turned.astype(BF16)

    def hw_copy(i, back):
        slot = lax.rem(d + nd - i, nd) if back else d
        return copy(hw_t.at[d], hw_t.at[slot], hw_s.at[i], hw_r.at[i], (lax.rem(d + i, nd), p))

    each(1, nd, lambda i: hw_copy(i, False).start())
    if done < half:
        ag_step(done)
        done += 1

    w_own.wait()
    w_copy.wait_recv()

    def forward(m):
        at_column = pl.multiple_of(m * 896, 128)
        columns = w2[:, :, pl.ds(at_column, 896)].reshape(2 * units, 896)
        part = jnp.dot(hw, columns, preferred_element_type=F32)
        for k in range(7):
            y_buf[pl.ds(m * 7 + k, toks, stride=tiles), :] = part[:, 128 * k:128 * k + 128]

    each(0, nd // 4, forward)
    if done < half:
        ag_step(done)
        done += 1
    each(nd // 4, nd // 2, forward)

    def y_at(t):
        return y_buf[pl.ds(pl.multiple_of((half - 1 - t) * 4 * tiles, 8), 4 * tiles), :]

    def rs_step(t):
        rs(t - 1).wait_recv()
        rs_out[t] = (y_at(t) + rs_in[t].astype(F32)).astype(BF16)
        rs(t).start()

    rs_out[0] = y_at(0).astype(BF16)
    rs(0).start()
    last = half - 1
    lag = done - 1
    split = max(1, half - 1 - lag)

    def both_steps(t):
        ag_step(t + lag)
        rs_step(t)

    each(1, split, both_steps)
    if done < half:
        ag_step(last)

    @pl.when(c == 0)
    def _():
        ag(last).wait_recv()

    def block_copy(i, back):
        to = lax.rem(d + i, nd)
        slot = lax.rem(d + nd - i, nd) if back else d
        return copy(ring.at[pl.ds(base, half), pl.ds(pl.multiple_of(16 * to, 16), 16), :], blocks.at[slot],
                    bl_s.at[i], bl_r.at[i], (to, p))

    each(1, nd, lambda i: block_copy(i, False).start())
    own_block = pltpu.make_async_copy(
        ring.at[pl.ds(base, half), pl.ds(pl.multiple_of(16 * d, 16), 16), :], blocks.at[d], local_sem.at[1])
    own_block.start()

    quarter = lax.broadcasted_iota(jnp.int32, (16 * half, 128), 0) & 3

    def spread(values, first):
        return [jnp.where(quarter == k, values, jnp.zeros_like(values)) for k in range(first, 4)]

    g_acc[...] = jnp.zeros_like(g_acc)

    def backward(m):
        at_column = pl.multiple_of(m * 896, 128)
        columns = w2[:, :, pl.ds(at_column, 896)].reshape(2 * units, 896)
        even = ring[pl.ds(base, half), pl.ds(pl.multiple_of(32 * m, 16), 16), :].reshape(16 * half, 128)
        odd = ring[pl.ds(base, half), pl.ds(pl.multiple_of(32 * m + 16, 16), 16), :].reshape(16 * half, 128)
        wide = jnp.concatenate(spread(even, 0) + spread(odd, 1), axis=1)
        g_acc[...] += lax.dot_general(wide, columns, NT, preferred_element_type=F32)

    rest = list(range(split, last))
    per = -(-(nd // 2) // max(1, len(rest) + 1))
    begun = 0
    for t in rest:
        rs_step(t)
        each(begun, min(begun + per, nd // 2), backward)
        begun = min(begun + per, nd // 2)

    rs(last - 1).wait_recv()

    @pl.when(c == 0)
    def _():
        rs_out[last] = (y_at(last) + rs_in[last].astype(F32)).astype(BF16)
        rs(last).start()

    @pl.when(c == 1)
    def _():
        fin[...] = y_at(last) + rs_in[last].astype(F32)

    each(begun, nd // 2, backward)

    @pl.when(c == 0)
    def _():
        rs(last).wait_recv()
        fin[...] = rs_in[last + 1].astype(F32)

    mix_copy = copy(fin.at[pl.ds(pl.multiple_of(2 * tiles * (1 - c), 8), 2 * tiles)], mix_in,
                    sib_s.at[3], sib_r.at[3], sibling)
    mix_copy.start()

    fours = onehot(lax.broadcasted_iota(jnp.int32, (toks, 16 * half), 0),
                   lax.broadcasted_iota(jnp.int32, (toks, 16 * half), 1) >> 2, F32)
    back = jnp.dot(fours, g_acc[...], preferred_element_type=F32, precision=lax.Precision.HIGHEST)
    slots = (keep * back + give * pltpu.roll(back, toks - 1, 0)).astype(BF16)
    home = place_of(lax.broadcasted_iota(jnp.int32, (4 * nz, toks), 1))
    home_row = lax.broadcasted_iota(jnp.int32, (4 * nz, toks), 0)
    placed = jnp.dot(onehot(home, home_row, BF16), slots, preferred_element_type=F32).astype(BF16)
    gh_send[...] = placed[:, units:]
    gh_copy = copy(gh_send, gh_in, sib_s.at[4], sib_r.at[4], sibling)
    gh_copy.start()

    repeat_row = lax.broadcasted_iota(jnp.int32, (2 * toks, 16 * half), 0)
    repeat_column = lax.broadcasted_iota(jnp.int32, (2 * toks, 16 * half), 1) >> 2
    repeat_own = onehot(repeat_row, repeat_column, BF16)
    repeat_sib = onehot(repeat_row, repeat_column + toks, BF16)

    def add_block(slot):
        left = jnp.concatenate([
            jnp.dot(hw_t[slot], repeat_own, preferred_element_type=F32),
            jnp.dot(hw_t[slot], repeat_sib, preferred_element_type=F32)], axis=0).astype(BF16)
        wide = jnp.concatenate(spread(blocks[slot].reshape(16 * half, 128), 0), axis=1)
        return jnp.dot(left, wide, preferred_element_type=F32)

    own_block.wait()
    acc[...] = add_block(d)

    def peer(i):
        hw_copy(i, True).wait_recv()
        block_copy(i, True).wait_recv()
        acc[...] += add_block(lax.rem(d + nd - i, nd))

    each(1, nd, peer)
    acc_copy = copy(acc.at[pl.ds(units, units)], acc_in, sib_s.at[5], sib_r.at[5], sibling)
    acc_copy.start()

    mix_copy.wait_recv()
    own_rows = fin[pl.ds(pl.multiple_of(2 * tiles * c, 8), 2 * tiles), :]
    mixed_ref[...] = (own_rows + mix_in[...]).astype(BF16)
    gh_copy.wait_recv()
    gh_ref[...] = (placed[:, :units].astype(F32) + gh_in[...].astype(F32)).astype(BF16)
    acc_copy.wait_recv()
    total = acc[pl.ds(0, units), :] + acc_in[...]
    gd_ref[...] = jnp.where(lax.rem(d, 2) == 1, total[:, 64:512], total[:, 0:448]).astype(BF16)

    for sent in (tok_copy, hid_copy, w_copy, mix_copy, gh_copy, acc_copy):
        sent.wait_send()
    each(1, radix, lambda i: one(i, False).wait_send())
    each(1, groups, lambda i: two(i, False).wait_send())
    each(0, last, lambda t: ag(t).wait_send())
    each(0, last, lambda t: rs(t).wait_send())

    @pl.when(c == 0)
    def _():
        ag(last).wait_send()
        rs(last).wait_send()

    each(1, nd, lambda i: hw_copy(i, False).wait_send())
    each(1, nd, lambda i: block_copy(i, False).wait_send())


def body(hidden, expert_ids, route_weight, cotangent, w_down):
    width = cotangent.shape[1]
    units = hidden.shape[1]
    nd, ne = lax.axis_size("dp"), lax.axis_size("expert")
    nz, half, tiles = ne // 2, ne // 4, width // 128
    toks = 4 * half
    radix = 8 if ne >= 64 else 4
    chosen = expert_ids[:, :, None] == jnp.arange(32, dtype=jnp.int32)
    named = jnp.any(chosen, axis=1)
    weight = jnp.sum(jnp.where(chosen, route_weight[:, :, None], 0.0), axis=1)
    zero = jnp.zeros_like(weight[0])
    keep = jnp.stack([weight[0], jnp.where(named[0], weight[1], zero)])
    moved = jnp.where(named[0], zero, weight[1])
    table = jnp.concatenate([keep, jnp.stack([zero, moved]), jnp.stack([moved, zero]), jnp.zeros((2, 32), F32)], axis=1)
    pieces = cotangent.reshape(2, nd // 2, 7, 128)
    pieces = jnp.stack([pieces[:, :, 0:4], pieces[:, :, 3:7]], axis=2).reshape(2, nd, 4, 128)
    tokens = pieces.transpose(1, 0, 2, 3).reshape(8 * nd, 128)
    vmem = pl.BlockSpec(memory_space=pltpu.VMEM)
    dma = lambda n: pltpu.SemaphoreType.DMA((n,))
    mixed, grad_hidden, grad_down = pl.pallas_call(
        functools.partial(kernel, nd, ne, radix),
        out_shape=(jax.ShapeDtypeStruct((2 * tiles, 128), BF16), jax.ShapeDtypeStruct((2 * ne, units), BF16),
                   jax.ShapeDtypeStruct((units, 448), BF16)),
        in_specs=[vmem, vmem, vmem, pl.BlockSpec(memory_space=pl.ANY)],
        out_specs=(vmem, vmem, vmem),
        scratch_shapes=[
            pltpu.VMEM((2, units, width), BF16),
            pltpu.VMEM((8 * nd, 128), BF16),
            pltpu.VMEM((nd, 16, 128), F32),
            pltpu.VMEM((2 * ne, units), BF16),
            pltpu.VMEM((ne, 2, 128), F32),
            pltpu.VMEM((2 * ne, 128), F32),
            pltpu.VMEM((half + 1, 16 * nd, 128), BF16),
            pltpu.VMEM((toks * tiles, 128), F32),
            pltpu.VMEM((half + 1, 4 * tiles, 128), BF16),
            pltpu.VMEM((half, 4 * tiles, 128), BF16),
            pltpu.VMEM((4 * tiles, 128), F32),
            pltpu.VMEM((2 * tiles, 128), F32),
            pltpu.VMEM((nd, units, 2 * toks), BF16),
            pltpu.VMEM((nd, half, 16, 128), BF16),
            pltpu.VMEM((16 * half, 2 * units), F32),
            pltpu.VMEM((2 * ne, units), BF16),
            pltpu.VMEM((2 * ne, units), BF16),
            pltpu.VMEM((2 * units, 512), F32),
            pltpu.VMEM((units, 512), F32),
            dma(2), dma(6), dma(6), dma(radix), dma(radix), dma(ne // radix), dma(ne // radix),
            dma(half), dma(half), dma(half), dma(half), dma(nd), dma(nd), dma(nd), dma(nd),
        ],
        compiler_params=pltpu.CompilerParams(collective_id=0, has_side_effects=True,
                                             vmem_limit_bytes=48 * 1024 * 1024),
        cost_estimate=pl.CostEstimate(flops=6 * 2 * ne * units * width, bytes_accessed=2 * units * width,
                                      transcendentals=0),
    )(tokens, hidden, table, w_down)
    return (mixed.reshape(2, width), grad_hidden, grad_down)


def solution(mesh):
    return jax.shard_map(
        body,
        mesh=mesh,
        in_specs=(
            P("dp", "expert"),
            P(("dp", "expert"), None),
            P(("dp", "expert"), None),
            P(("dp", "expert"), None),
            P("expert", None),
        ),
        out_specs=(P(("dp", "expert"), None), P("dp", "expert"), P("expert", "dp")),
        check_vma=False,
    )
```

```python
import functools

import jax
import jax.numpy as jnp
from jax import lax
from jax.experimental import pallas as pl
from jax.experimental.pallas import tpu as pltpu
from jax.sharding import PartitionSpec as P

MESH = pl.DeviceIdType.MESH
F32, BF16 = jnp.float32, jnp.bfloat16
NT = (((1,), (1,)), ((), ()))
TN = (((0,), (0,)), ((), ()))
LAG = 4


def onehot(rows, columns, dtype):
    return (rows == columns).astype(F32).astype(dtype)


def kernel(nd, ne, leap, ids_ref, weight_ref, cot_ref, hid_ref, w_ref, mixed_ref, gh_ref, gd_ref,
           w2, ids, weights, cot, own_half, sib_half, own_hid, sib_hid, own_tab, sib_tab, table, flat, ring,
           y_buf, rs_in, rs_out, fin, mix_in, hw_t, blocks, g_acc, gh_send, gh_in, acc, acc_in,
           local_sem, sib_s, sib_r, tab_s, tab_r, ag_s, ag_r, rs_s, rs_r, hw_s, hw_r, bl_s, bl_r):
    nz, half = ne // 2, ne // 4
    toks = 4 * half
    reach = half // 2
    units = hid_ref.shape[1]
    tiles = w2.shape[2] // 128
    d, p = lax.axis_index("dp"), lax.axis_index("expert")
    z, c = p // 2, lax.rem(p, 2)
    way = 1 - 2 * c
    expert = p // 4
    base = 1 - c
    sibling = (d, p + 1 - 2 * c)

    def chip(steps):
        return (d, lax.rem(z + way * steps + 2 * nz, nz) * 2 + c)

    def copy(src, dst, send, recv, to):
        return pltpu.make_async_remote_copy(src_ref=src, dst_ref=dst, send_sem=send, recv_sem=recv,
                                            device_id=to, device_id_type=MESH)

    def each(low, high, step):
        def run(i, _):
            step(i)
            return 0
        lax.fori_loop(low, high, run, 0)

    loads = [pltpu.make_async_copy(a, b, local_sem.at[i]) for i, (a, b) in enumerate(
        ((ids_ref, ids), (weight_ref, weights), (cot_ref, cot), (hid_ref, own_hid), (w_ref, w2.at[0])))]
    for load in loads:
        load.start()

    barrier = pltpu.get_barrier_semaphore()

    def greet(to):
        pl.semaphore_signal(barrier, inc=1, device_id=to, device_id_type=MESH)

    greet(sibling)
    each(1, reach + 1, lambda i: greet(chip(-i)))
    greet(chip(-leap))
    greet(chip(1))
    greet(chip(leap))
    each(1, nd, lambda i: greet((lax.rem(d + i, nd), p)))

    loads[0].wait()
    loads[1].wait()
    lane = lax.broadcasted_iota(jnp.int32, (1, 128), 1)
    named = [jnp.zeros((1, 128), F32), jnp.zeros((1, 128), F32)]
    weight = [jnp.zeros((1, 128), F32), jnp.zeros((1, 128), F32)]
    for k in range(ids.shape[1]):
        for t in range(2):
            hit = ids[t:t + 1, k:k + 1] == (lane & 31)
            named[t] = jnp.where(hit, 1.0, named[t])
            weight[t] = jnp.where(hit, weights[t:t + 1, k:k + 1], weight[t])
    part = lane >> 5
    moved = jnp.where(named[0] > 0, 0.0, weight[1])
    kept = jnp.where(named[0] > 0, weight[1], 0.0)
    zero = jnp.zeros_like(moved)
    own_tab[0:1, :] = jnp.where(part == 0, weight[0], jnp.where(part == 2, moved, zero))
    own_tab[1:2, :] = jnp.where(part == 0, kept, jnp.where(part == 1, moved, zero))
    loads[2].wait()
    for block in range(nd):
        for q in range(4):
            tile = (block // 2) * 7 + 3 * (block % 2) + q
            own_half[pl.ds(8 * block + q, 2, stride=4), :] = cot[:, 128 * tile:128 * tile + 128].astype(F32)
    loads[3].wait()
    pl.semaphore_wait(barrier, 4 + reach + nd - 1)

    tab_copy = copy(own_tab, sib_tab, sib_s.at[6], sib_r.at[6], sibling)
    tok_copy = copy(own_half, sib_half, sib_s.at[0], sib_r.at[0], sibling)
    hid_copy = copy(own_hid, sib_hid, sib_s.at[1], sib_r.at[1], sibling)
    w_copy = copy(w_ref, w2.at[1], sib_s.at[2], sib_r.at[2], sibling)
    tab_copy.start()
    tok_copy.start()
    hid_copy.start()

    def tab(r, first):
        slot = first + r
        return copy(table.at[first], table.at[slot], tab_s.at[slot], tab_r.at[slot], chip(r))

    def ag(s):
        return copy(ring.at[s], ring.at[s + 1], ag_s.at[s], ag_r.at[s + 1], chip(1))

    ag_leap = copy(ring.at[0], ring.at[leap], ag_s.at[leap - 1], ag_r.at[leap], chip(leap))

    def ag_landed(s):
        copy(ring.at[0], ring.at[s], ag_s.at[0], ag_r.at[s], chip(1)).wait_recv()

    def near_step(s):
        ag_landed(s)
        ag(s).start()

    def far_step(s):
        ag_landed(s)
        if isinstance(s, int) and s == half - 1:
            @pl.when(c == 0)
            def _():
                ag(s).start()
        else:
            ag(s).start()

    def rounds(low, high):
        for s in range(low, high):
            if s < leap - 1:
                near_step(s)
            far = leap + s - late
            if leap <= far < half:
                far_step(far)

    tab_copy.wait_recv()
    mine, theirs = own_tab[...], sib_tab[...]
    first = c == 0
    table[0] = jnp.concatenate([jnp.where(first, mine, theirs), jnp.where(first, theirs, mine)], axis=0)
    each(0, reach, lambda i: tab(reach - i, 0).start())
    tok_copy.wait_recv()
    mine, theirs = own_half[...].reshape(nd, 8, 128), sib_half[...].reshape(nd, 8, 128)
    ring[0] = jnp.concatenate([jnp.where(first, mine, theirs), jnp.where(first, theirs, mine)],
                              axis=1).reshape(16 * nd, 128).astype(BF16)
    late = max(1, 2 * leap - 1 - half)
    ag(0).start()
    ag_leap.start()
    w_copy.start()
    top = max(leap - 1, half - leap + late)
    rounds(1, min(3, top))
    tab(reach, 0).wait_recv()
    each(0, reach, lambda i: tab(reach - i, reach).start())
    rounds(3, min(5, top))
    each(1, reach, lambda i: tab(i, 0).wait_recv())
    each(1, reach + 1, lambda i: tab(i, reach).wait_recv())
    hid_copy.wait_recv()

    for i in range(half):
        flat[4 * i:4 * i + 4, :] = table[base + i]
    row = lax.broadcasted_iota(jnp.int32, (toks, 4 * nz), 0)
    column = lax.broadcasted_iota(jnp.int32, (toks, 4 * nz), 1)

    def place_of(token):
        at = z - way * ((token >> 2) + base)
        at = jnp.where(at < 0, at + nz, at)
        at = jnp.where(at >= nz, at - nz, at)
        return at * 4 + (token & 3)

    place = place_of(row)
    picked = flat[...]
    lanes = lax.broadcasted_iota(jnp.int32, (toks, 128), 1)

    def coefficient(k):
        return jnp.sum(jnp.where(lanes == expert + 32 * k, picked, 0.0), axis=1, keepdims=True)

    keep, shift, give = coefficient(0), coefficient(1), coefficient(2)
    both = jnp.concatenate([own_hid[...], sib_hid[...]], axis=1)
    at = jnp.dot(onehot(place, column, BF16), both, preferred_element_type=F32)
    before = jnp.dot(onehot(place - 1, column, BF16), both, preferred_element_type=F32)
    hw = (keep * at + shift * before).astype(BF16)

    loads[4].wait()
    w_copy.wait_recv()

    def forward(m):
        at_column = pl.multiple_of(m * 896, 128)
        columns = w2[:, :, pl.ds(at_column, 896)].reshape(2 * units, 896)
        part = jnp.dot(hw, columns, preferred_element_type=F32)
        for k in range(7):
            y_buf[pl.ds(m * 7 + k, toks, stride=tiles), :] = part[:, 128 * k:128 * k + 128]

    each(0, nd // 2, forward)

    def y_at(s):
        return y_buf[pl.ds(pl.multiple_of((s - base) * 4 * tiles, 8), 4 * tiles), :]

    def rs(s):
        return copy(rs_out.at[s], rs_in.at[s - 1], rs_s.at[s], rs_r.at[s - 1], chip(-1))

    rs_leap = copy(rs_out.at[leap], rs_in.at[leap - 1], rs_s.at[leap], rs_r.at[leap - 1], chip(-leap))

    def rs_landed(s):
        copy(rs_out.at[0], rs_in.at[s], rs_s.at[0], rs_r.at[s], chip(-1)).wait_recv()

    def rs_add(s):
        rs_landed(s)
        rs_out[s] = (y_at(s) + rs_in[s].astype(F32)).astype(BF16)

    last = half - 1

    @pl.when(first)
    def _():
        rs_out[half] = y_at(half).astype(BF16)
        rs(half).start()

    rs_out[leap - 1] = y_at(leap - 1).astype(BF16)
    rs(leap - 1).start()
    rounds(5, min(6, top))

    spot_row = lax.broadcasted_iota(jnp.int32, (toks, 2 * toks), 0)
    spot_column = lax.broadcasted_iota(jnp.int32, (toks, 2 * toks), 1)
    turned = lax.dot_general(hw[:, :units], onehot(spot_row, spot_column, BF16), TN, preferred_element_type=F32)
    turned = turned + lax.dot_general(hw[:, units:], onehot(spot_row + toks, spot_column, BF16), TN,
                                      preferred_element_type=F32)
    hw_t[d] = turned.astype(BF16)

    def hw_copy(i, back):
        slot = lax.rem(d + nd - i, nd) if back else d
        return copy(hw_t.at[d], hw_t.at[slot], hw_s.at[i], hw_r.at[i], (lax.rem(d + i, nd), p))

    each(1, nd, lambda i: hw_copy(i, False).start())

    @pl.when(first)
    def _():
        rs_add(last)

    @pl.when(c == 1)
    def _():
        rs_out[last] = y_at(last).astype(BF16)

    def rs_send(s):
        if s == leap:
            rs_leap.start()
        else:
            rs(s).start()

    rs_send(last)
    far_left = list(range(last - 1, leap - 1, -1))
    near_left = list(range(leap - 2, 0, -1))
    order = []
    while far_left or near_left:
        if near_left:
            order.append(near_left.pop(0))
        if far_left:
            order.append(far_left.pop(0))

    def block_copy(i, back):
        to = lax.rem(d + i, nd)
        slot = lax.rem(d + nd - i, nd) if back else d
        return copy(ring.at[pl.ds(base, half), pl.ds(pl.multiple_of(16 * to, 16), 16), :], blocks.at[slot],
                    bl_s.at[i], bl_r.at[i], (to, p))

    own_block = pltpu.make_async_copy(
        ring.at[pl.ds(base, half), pl.ds(pl.multiple_of(16 * d, 16), 16), :], blocks.at[d], local_sem.at[5])
    quarter = lax.broadcasted_iota(jnp.int32, (16 * half, 128), 0) & 3

    def spread(values, low):
        return [jnp.where(quarter == k, values, jnp.zeros_like(values)) for k in range(low, 4)]

    g_acc[...] = jnp.zeros_like(g_acc)

    def backward(m):
        at_column = pl.multiple_of(m * 896, 128)
        columns = w2[:, :, pl.ds(at_column, 896)].reshape(2 * units, 896)
        even = ring[pl.ds(base, half), pl.ds(pl.multiple_of(32 * m, 16), 16), :].reshape(16 * half, 128)
        odd = ring[pl.ds(base, half), pl.ds(pl.multiple_of(32 * m + 16, 16), 16), :].reshape(16 * half, 128)
        wide = jnp.concatenate(spread(even, 0) + spread(odd, 1), axis=1)
        g_acc[...] += lax.dot_general(wide, columns, NT, preferred_element_type=F32)

    begun = 0
    going = 6
    gathered = False
    for count, s in enumerate(order):
        rs_add(s)
        rs_send(s)
        if count % 2 == 1 or count == len(order) - 1:
            if going < top:
                rounds(going, going + 1)
                going += 1
            elif not gathered:
                gathered = True

                @pl.when(first)
                def _():
                    ag_landed(half)

                if leap > 1:
                    ag_landed(leap - 1)
                each(1, nd, lambda i: block_copy(i, False).start())
                own_block.start()
        if gathered and begun < nd // 2:
            stop = min(begun + max(1, nd // 8), nd // 2)
            each(begun, stop, backward)
            begun = stop
    assert gathered
    each(begun, nd // 2, backward)

    fours = onehot(lax.broadcasted_iota(jnp.int32, (toks, 16 * half), 0),
                   lax.broadcasted_iota(jnp.int32, (toks, 16 * half), 1) >> 2, F32)
    back = jnp.dot(fours, g_acc[...], preferred_element_type=F32, precision=lax.Precision.HIGHEST)
    slots = (keep * back + give * pltpu.roll(back, toks - 1, 0)).astype(BF16)
    home = place_of(lax.broadcasted_iota(jnp.int32, (4 * nz, toks), 1))
    home_row = lax.broadcasted_iota(jnp.int32, (4 * nz, toks), 0)
    placed = jnp.dot(onehot(home, home_row, BF16), slots, preferred_element_type=F32).astype(BF16)
    gh_send[...] = placed[:, units:]
    gh_copy = copy(gh_send, gh_in, sib_s.at[4], sib_r.at[4], sibling)
    gh_copy.start()

    rs_landed(0)
    rs_landed(leap - 1)
    arrived = rs_in[0].astype(F32) + rs_in[leap - 1].astype(F32)

    @pl.when(first)
    def _():
        fin[...] = arrived

    @pl.when(c == 1)
    def _():
        fin[...] = arrived + y_at(0)

    mix_copy = copy(fin.at[pl.ds(pl.multiple_of(2 * tiles * (1 - c), 8), 2 * tiles)], mix_in,
                    sib_s.at[3], sib_r.at[3], sibling)
    mix_copy.start()

    repeat_row = lax.broadcasted_iota(jnp.int32, (2 * toks, 16 * half), 0)
    repeat_column = lax.broadcasted_iota(jnp.int32, (2 * toks, 16 * half), 1) >> 2
    repeat_own = onehot(repeat_row, repeat_column, BF16)
    repeat_sib = onehot(repeat_row, repeat_column + toks, BF16)

    def add_block(slot):
        left = jnp.concatenate([
            jnp.dot(hw_t[slot], repeat_own, preferred_element_type=F32),
            jnp.dot(hw_t[slot], repeat_sib, preferred_element_type=F32)], axis=0).astype(BF16)
        wide = jnp.concatenate(spread(blocks[slot].reshape(16 * half, 128), 0), axis=1)
        return jnp.dot(left, wide, preferred_element_type=F32)

    own_block.wait()
    acc[...] = add_block(d)

    def peer(i):
        hw_copy(i, True).wait_recv()
        block_copy(i, True).wait_recv()
        acc[...] += add_block(lax.rem(d + nd - i, nd))

    each(1, nd, peer)
    acc_copy = copy(acc.at[pl.ds(units, units)], acc_in, sib_s.at[5], sib_r.at[5], sibling)
    acc_copy.start()

    mix_copy.wait_recv()
    own_rows = fin[pl.ds(pl.multiple_of(2 * tiles * c, 8), 2 * tiles), :]
    mixed_ref[...] = (own_rows + mix_in[...]).astype(BF16)
    gh_copy.wait_recv()
    gh_ref[...] = (placed[:, :units].astype(F32) + gh_in[...].astype(F32)).astype(BF16)
    acc_copy.wait_recv()
    total = acc[pl.ds(0, units), :] + acc_in[...]
    gd_ref[...] = jnp.where(lax.rem(d, 2) == 1, total[:, 64:512], total[:, 0:448]).astype(BF16)

    for sent in (tab_copy, tok_copy, hid_copy, w_copy, mix_copy, gh_copy, acc_copy, ag_leap, rs_leap):
        sent.wait_send()
    each(1, reach + 1, lambda i: tab(i, 0).wait_send())
    each(1, reach + 1, lambda i: tab(i, reach).wait_send())
    each(0, leap - 1, lambda s: ag(s).wait_send())
    each(leap, last, lambda s: ag(s).wait_send())
    each(1, leap, lambda s: rs(s).wait_send())
    each(leap + 1, half, lambda s: rs(s).wait_send())

    @pl.when(first)
    def _():
        ag(last).wait_send()
        rs(half).wait_send()

    each(1, nd, lambda i: hw_copy(i, False).wait_send())
    each(1, nd, lambda i: block_copy(i, False).wait_send())


def body(hidden, expert_ids, route_weight, cotangent, w_down):
    width = cotangent.shape[1]
    units = hidden.shape[1]
    nd, ne = lax.axis_size("dp"), lax.axis_size("expert")
    half, tiles = ne // 4, width // 128
    leap = 5 * half // 8
    toks = 4 * half
    vmem = pl.BlockSpec(memory_space=pltpu.VMEM)
    anywhere = pl.BlockSpec(memory_space=pl.ANY)
    dma = lambda n: pltpu.SemaphoreType.DMA((n,))
    mixed, grad_hidden, grad_down = pl.pallas_call(
        functools.partial(kernel, nd, ne, leap),
        out_shape=(jax.ShapeDtypeStruct((2 * tiles, 128), BF16), jax.ShapeDtypeStruct((2 * ne, units), BF16),
                   jax.ShapeDtypeStruct((units, 448), BF16)),
        in_specs=[anywhere] * 5,
        out_specs=(vmem, vmem, vmem),
        scratch_shapes=[
            pltpu.VMEM((2, units, width), BF16),
            pltpu.VMEM(expert_ids.shape, jnp.int32),
            pltpu.VMEM(route_weight.shape, F32),
            pltpu.VMEM(cotangent.shape, BF16),
            pltpu.VMEM((8 * nd, 128), F32),
            pltpu.VMEM((8 * nd, 128), F32),
            pltpu.VMEM((2 * ne, units), BF16),
            pltpu.VMEM((2 * ne, units), BF16),
            pltpu.VMEM((2, 128), F32),
            pltpu.VMEM((2, 128), F32),
            pltpu.VMEM((half + 1, 4, 128), F32),
            pltpu.VMEM((toks, 128), F32),
            pltpu.VMEM((half + 1, 16 * nd, 128), BF16),
            pltpu.VMEM((toks * tiles, 128), F32),
            pltpu.VMEM((half, 4 * tiles, 128), BF16),
            pltpu.VMEM((half + 1, 4 * tiles, 128), BF16),
            pltpu.VMEM((4 * tiles, 128), F32),
            pltpu.VMEM((2 * tiles, 128), F32),
            pltpu.VMEM((nd, units, 2 * toks), BF16),
            pltpu.VMEM((nd, half, 16, 128), BF16),
            pltpu.VMEM((16 * half, 2 * units), F32),
            pltpu.VMEM((2 * ne, units), BF16),
            pltpu.VMEM((2 * ne, units), BF16),
            pltpu.VMEM((2 * units, 512), F32),
            pltpu.VMEM((units, 512), F32),
            dma(6), dma(7), dma(7), dma(half + 1), dma(half + 1), dma(half), dma(half + 1), dma(half + 1), dma(half),
            dma(nd), dma(nd), dma(nd), dma(nd),
        ],
        compiler_params=pltpu.CompilerParams(collective_id=0, has_side_effects=True,
                                             vmem_limit_bytes=56 * 1024 * 1024),
        cost_estimate=pl.CostEstimate(flops=12 * ne * units * width, bytes_accessed=2 * units * width,
                                      transcendentals=0),
    )(expert_ids, route_weight, cotangent, hidden, w_down)
    return (mixed.reshape(2, width), grad_hidden, grad_down)


def solution(mesh):
    return jax.shard_map(
        body,
        mesh=mesh,
        in_specs=(
            P("dp", "expert"),
            P(("dp", "expert"), None),
            P(("dp", "expert"), None),
            P(("dp", "expert"), None),
            P("expert", None),
        ),
        out_specs=(P(("dp", "expert"), None), P("dp", "expert"), P("expert", "dp")),
        check_vma=False,
    )
```

```python
import functools

import jax
import jax.numpy as jnp
from jax import lax
from jax.experimental import pallas as pl
from jax.experimental.pallas import tpu as pltpu
from jax.sharding import PartitionSpec as P

MESH = pl.DeviceIdType.MESH
F32, BF16 = jnp.float32, jnp.bfloat16
NT = (((1,), (1,)), ((), ()))
TN = (((0,), (0,)), ((), ()))
LAG = 4


def onehot(rows, columns, dtype):
    return (rows == columns).astype(F32).astype(dtype)


def kernel(nd, ne, leap, ids_ref, weight_ref, cot_ref, hid_ref, w_ref, mixed_ref, gh_ref, gd_ref,
           w2, ids, weights, cot, own_half, sib_half, own_hid, sib_hid, own_tab, sib_tab, table, flat, ring,
           y_buf, rs_in, rs_out, fin, mix_in, hw_t, lefts, blocks, g_acc, gh_send, gh_in, acc, acc_in,
           local_sem, sib_s, sib_r, tab_s, tab_r, ag_s, ag_r, rs_s, rs_r, hw_s, hw_r, bl_s, bl_r):
    nz, half = ne // 2, ne // 4
    toks = 4 * half
    reach = half // 2
    units = hid_ref.shape[1]
    tiles = w2.shape[2] // 128
    d, p = lax.axis_index("dp"), lax.axis_index("expert")
    z, c = p // 2, lax.rem(p, 2)
    way = 1 - 2 * c
    expert = p // 4
    base = 1 - c
    sibling = (d, p + 1 - 2 * c)

    def chip(steps):
        return (d, lax.rem(z + way * steps + 2 * nz, nz) * 2 + c)

    def copy(src, dst, send, recv, to):
        return pltpu.make_async_remote_copy(src_ref=src, dst_ref=dst, send_sem=send, recv_sem=recv,
                                            device_id=to, device_id_type=MESH)

    def each(low, high, step):
        def run(i, _):
            step(i)
            return 0
        lax.fori_loop(low, high, run, 0)

    loads = [pltpu.make_async_copy(a, b, local_sem.at[i]) for i, (a, b) in enumerate(
        ((ids_ref, ids), (weight_ref, weights), (cot_ref, cot), (hid_ref, own_hid), (w_ref, w2.at[0])))]
    for load in loads:
        load.start()

    barrier = pltpu.get_barrier_semaphore()

    def greet(to):
        pl.semaphore_signal(barrier, inc=1, device_id=to, device_id_type=MESH)

    greet(sibling)
    each(1, reach + 1, lambda i: greet(chip(-i)))
    greet(chip(-leap))
    greet(chip(1))
    greet(chip(leap))
    each(1, nd, lambda i: greet((lax.rem(d + i, nd), p)))

    loads[0].wait()
    loads[1].wait()
    lane = lax.broadcasted_iota(jnp.int32, (1, 128), 1)
    named = [jnp.zeros((1, 128), F32), jnp.zeros((1, 128), F32)]
    weight = [jnp.zeros((1, 128), F32), jnp.zeros((1, 128), F32)]
    for k in range(ids.shape[1]):
        for t in range(2):
            hit = ids[t:t + 1, k:k + 1] == (lane & 31)
            named[t] = jnp.where(hit, 1.0, named[t])
            weight[t] = jnp.where(hit, weights[t:t + 1, k:k + 1], weight[t])
    part = lane >> 5
    moved = jnp.where(named[0] > 0, 0.0, weight[1])
    kept = jnp.where(named[0] > 0, weight[1], 0.0)
    zero = jnp.zeros_like(moved)
    own_tab[0:1, :] = jnp.where(part == 0, weight[0], jnp.where(part == 2, moved, zero))
    own_tab[1:2, :] = jnp.where(part == 0, kept, jnp.where(part == 1, moved, zero))
    pl.semaphore_wait(barrier, 4 + reach + nd - 1)

    tab_copy = copy(own_tab, sib_tab, sib_s.at[6], sib_r.at[6], sibling)
    tok_copy = copy(own_half, sib_half, sib_s.at[0], sib_r.at[0], sibling)
    hid_copy = copy(own_hid, sib_hid, sib_s.at[1], sib_r.at[1], sibling)
    w_copy = copy(w_ref, w2.at[1], sib_s.at[2], sib_r.at[2], sibling)
    tab_copy.start()
    loads[2].wait()
    for block in range(nd):
        for q in range(4):
            tile = (block // 2) * 7 + 3 * (block % 2) + q
            own_half[pl.ds(8 * block + q, 2, stride=4), :] = cot[:, 128 * tile:128 * tile + 128].astype(F32)
    tok_copy.start()

    def tab(r, first):
        slot = first + r
        return copy(table.at[first], table.at[slot], tab_s.at[slot], tab_r.at[slot], chip(r))

    def ag(s):
        return copy(ring.at[s], ring.at[s + 1], ag_s.at[s], ag_r.at[s + 1], chip(1))

    ag_leap = copy(ring.at[0], ring.at[leap], ag_s.at[leap - 1], ag_r.at[leap], chip(leap))

    def ag_landed(s):
        copy(ring.at[0], ring.at[s], ag_s.at[0], ag_r.at[s], chip(1)).wait_recv()

    def near_step(s):
        ag_landed(s)
        ag(s).start()

    def far_step(s):
        ag_landed(s)
        if isinstance(s, int) and s == half - 1:
            @pl.when(c == 0)
            def _():
                ag(s).start()
        else:
            ag(s).start()

    def rounds(low, high):
        for s in range(low, high):
            if s < leap - 1:
                near_step(s)
            far = leap + s - late
            if leap <= far < half:
                far_step(far)

    tab_copy.wait_recv()
    mine, theirs = own_tab[...], sib_tab[...]
    first = c == 0
    table[0] = jnp.concatenate([jnp.where(first, mine, theirs), jnp.where(first, theirs, mine)], axis=0)
    each(0, reach, lambda i: tab(reach - i, 0).start())
    loads[3].wait()
    hid_copy.start()
    tok_copy.wait_recv()
    mine, theirs = own_half[...].reshape(nd, 8, 128), sib_half[...].reshape(nd, 8, 128)
    ring[0] = jnp.concatenate([jnp.where(first, mine, theirs), jnp.where(first, theirs, mine)],
                              axis=1).reshape(16 * nd, 128).astype(BF16)
    late = max(1, 2 * leap - 1 - half)
    ag(0).start()
    ag_leap.start()
    w_copy.start()
    top = max(leap - 1, half - leap + late)
    rounds(1, min(2, top))
    tab(reach, 0).wait_recv()
    each(0, reach, lambda i: tab(reach - i, reach).start())
    rounds(2, min(4, top))
    each(1, reach, lambda i: tab(i, 0).wait_recv())
    each(1, reach + 1, lambda i: tab(i, reach).wait_recv())
    hid_copy.wait_recv()

    for i in range(half):
        flat[4 * i:4 * i + 4, :] = table[base + i]
    row = lax.broadcasted_iota(jnp.int32, (toks, 4 * nz), 0)
    column = lax.broadcasted_iota(jnp.int32, (toks, 4 * nz), 1)

    def place_of(token):
        at = z - way * ((token >> 2) + base)
        at = jnp.where(at < 0, at + nz, at)
        at = jnp.where(at >= nz, at - nz, at)
        return at * 4 + (token & 3)

    place = place_of(row)
    picked = flat[...]
    lanes = lax.broadcasted_iota(jnp.int32, (toks, 128), 1)

    def coefficient(k):
        return jnp.sum(jnp.where(lanes == expert + 32 * k, picked, 0.0), axis=1, keepdims=True)

    keep, shift, give = coefficient(0), coefficient(1), coefficient(2)
    both = jnp.concatenate([own_hid[...], sib_hid[...]], axis=1)
    at = jnp.dot(onehot(place, column, BF16), both, preferred_element_type=F32)
    before = jnp.dot(onehot(place - 1, column, BF16), both, preferred_element_type=F32)
    hw = (keep * at + shift * before).astype(BF16)

    loads[4].wait()
    w_copy.wait_recv()

    def forward(m):
        at_column = pl.multiple_of(m * 896, 128)
        columns = w2[:, :, pl.ds(at_column, 896)].reshape(2 * units, 896)
        part = jnp.dot(hw, columns, preferred_element_type=F32)
        for k in range(7):
            y_buf[pl.ds(m * 7 + k, toks, stride=tiles), :] = part[:, 128 * k:128 * k + 128]

    each(0, nd // 2, forward)

    def y_at(s):
        return y_buf[pl.ds(pl.multiple_of((s - base) * 4 * tiles, 8), 4 * tiles), :]

    def rs(s):
        return copy(rs_out.at[s], rs_in.at[s - 1], rs_s.at[s], rs_r.at[s - 1], chip(-1))

    rs_leap = copy(rs_out.at[leap], rs_in.at[leap - 1], rs_s.at[leap], rs_r.at[leap - 1], chip(-leap))

    def rs_landed(s):
        copy(rs_out.at[0], rs_in.at[s], rs_s.at[0], rs_r.at[s], chip(-1)).wait_recv()

    def rs_add(s):
        rs_landed(s)
        rs_out[s] = (y_at(s) + rs_in[s].astype(F32)).astype(BF16)

    last = half - 1

    @pl.when(first)
    def _():
        rs_out[half] = y_at(half).astype(BF16)
        rs(half).start()

    rs_out[leap - 1] = y_at(leap - 1).astype(BF16)
    rs(leap - 1).start()
    rounds(4, min(6, top))

    spot_row = lax.broadcasted_iota(jnp.int32, (toks, 2 * toks), 0)
    spot_column = lax.broadcasted_iota(jnp.int32, (toks, 2 * toks), 1)
    turned = lax.dot_general(hw[:, :units], onehot(spot_row, spot_column, BF16), TN, preferred_element_type=F32)
    turned = turned + lax.dot_general(hw[:, units:], onehot(spot_row + toks, spot_column, BF16), TN,
                                      preferred_element_type=F32)
    hw_t[d] = turned.astype(BF16)

    def hw_copy(i, back):
        slot = lax.rem(d + nd - i, nd) if back else d
        return copy(hw_t.at[d], hw_t.at[slot], hw_s.at[i], hw_r.at[i], (lax.rem(d + i, nd), p))

    each(1, nd, lambda i: hw_copy(i, False).start())

    @pl.when(first)
    def _():
        rs_add(last)

    @pl.when(c == 1)
    def _():
        rs_out[last] = y_at(last).astype(BF16)

    def rs_send(s):
        if s == leap:
            rs_leap.start()
        else:
            rs(s).start()

    rs_send(last)
    far_left = list(range(last - 1, leap - 1, -1))
    near_left = list(range(leap - 2, 0, -1))
    order = []
    while far_left or near_left:
        if near_left:
            order.append(near_left.pop(0))
        if far_left:
            order.append(far_left.pop(0))

    def block_copy(i, back):
        to = lax.rem(d + i, nd)
        slot = lax.rem(d + nd - i, nd) if back else d
        return copy(ring.at[pl.ds(base, half), pl.ds(pl.multiple_of(16 * to, 16), 16), :], blocks.at[slot],
                    bl_s.at[i], bl_r.at[i], (to, p))

    own_block = pltpu.make_async_copy(
        ring.at[pl.ds(base, half), pl.ds(pl.multiple_of(16 * d, 16), 16), :], blocks.at[d], local_sem.at[5])
    quarter = lax.broadcasted_iota(jnp.int32, (16 * half, 128), 0) & 3

    def spread(values, low):
        return [jnp.where(quarter == k, values, jnp.zeros_like(values)) for k in range(low, 4)]

    g_acc[...] = jnp.zeros_like(g_acc)

    def backward(m):
        at_column = pl.multiple_of(m * 896, 128)
        columns = w2[:, :, pl.ds(at_column, 896)].reshape(2 * units, 896)
        even = ring[pl.ds(base, half), pl.ds(pl.multiple_of(32 * m, 16), 16), :].reshape(16 * half, 128)
        odd = ring[pl.ds(base, half), pl.ds(pl.multiple_of(32 * m + 16, 16), 16), :].reshape(16 * half, 128)
        wide = jnp.concatenate(spread(even, 0) + spread(odd, 1), axis=1)
        g_acc[...] += lax.dot_general(wide, columns, NT, preferred_element_type=F32)

    repeat_row = lax.broadcasted_iota(jnp.int32, (2 * toks, 16 * half), 0)
    repeat_column = lax.broadcasted_iota(jnp.int32, (2 * toks, 16 * half), 1) >> 2
    repeat_own = onehot(repeat_row, repeat_column, BF16)
    repeat_sib = onehot(repeat_row, repeat_column + toks, BF16)

    def make_left(slot):
        lefts[slot] = jnp.concatenate([
            jnp.dot(hw_t[slot], repeat_own, preferred_element_type=F32),
            jnp.dot(hw_t[slot], repeat_sib, preferred_element_type=F32)], axis=0).astype(BF16)

    def peer_left(i):
        hw_copy(i, True).wait_recv()
        make_left(lax.rem(d + nd - i, nd))

    begun = 0
    going = 6
    gathered = False
    for count, s in enumerate(order):
        rs_add(s)
        rs_send(s)
        if count % 2 == 1 or count == len(order) - 1:
            if going < top:
                rounds(going, going + 1)
                going += 1
            elif not gathered:
                gathered = True

                @pl.when(first)
                def _():
                    ag_landed(half)

                if leap > 1:
                    ag_landed(leap - 1)
                each(1, nd, lambda i: block_copy(i, False).start())
                own_block.start()
        if gathered and begun < nd // 2:
            stop = min(begun + max(1, nd // 8), nd // 2)
            each(begun, stop, backward)
            begun = stop
        if count == len(order) - 2:
            make_left(d)
            each(1, nd // 2, peer_left)
        if count == len(order) - 1:
            if len(order) < 2:
                make_left(d)
                each(1, nd // 2, peer_left)
            each(nd // 2, nd, peer_left)
    assert gathered
    each(begun, nd // 2, backward)

    fours = onehot(lax.broadcasted_iota(jnp.int32, (toks, 16 * half), 0),
                   lax.broadcasted_iota(jnp.int32, (toks, 16 * half), 1) >> 2, F32)
    back = jnp.dot(fours, g_acc[...], preferred_element_type=F32, precision=lax.Precision.HIGHEST)
    slots = (keep * back + give * pltpu.roll(back, toks - 1, 0)).astype(BF16)
    home = place_of(lax.broadcasted_iota(jnp.int32, (4 * nz, toks), 1))
    home_row = lax.broadcasted_iota(jnp.int32, (4 * nz, toks), 0)
    placed = jnp.dot(onehot(home, home_row, BF16), slots, preferred_element_type=F32).astype(BF16)
    gh_send[...] = placed[:, units:]
    gh_copy = copy(gh_send, gh_in, sib_s.at[4], sib_r.at[4], sibling)
    gh_copy.start()

    def add_block(slot):
        wide = jnp.concatenate(spread(blocks[slot].reshape(16 * half, 128), 0), axis=1)
        return jnp.dot(lefts[slot], wide, preferred_element_type=F32)

    own_block.wait()
    acc[...] = add_block(d)

    def peer(i):
        block_copy(i, True).wait_recv()
        acc[...] += add_block(lax.rem(d + nd - i, nd))

    each(1, nd, peer)
    acc_copy = copy(acc.at[pl.ds(units, units)], acc_in, sib_s.at[5], sib_r.at[5], sibling)
    acc_copy.start()

    rs_landed(0)
    rs_landed(leap - 1)
    arrived = rs_in[0].astype(F32) + rs_in[leap - 1].astype(F32)

    @pl.when(first)
    def _():
        fin[...] = arrived

    @pl.when(c == 1)
    def _():
        fin[...] = arrived + y_at(0)

    mix_copy = copy(fin.at[pl.ds(pl.multiple_of(2 * tiles * (1 - c), 8), 2 * tiles)], mix_in,
                    sib_s.at[3], sib_r.at[3], sibling)
    mix_copy.start()

    mix_copy.wait_recv()
    own_rows = fin[pl.ds(pl.multiple_of(2 * tiles * c, 8), 2 * tiles), :]
    mixed_ref[...] = (own_rows + mix_in[...]).astype(BF16)
    gh_copy.wait_recv()
    gh_ref[...] = (placed[:, :units].astype(F32) + gh_in[...].astype(F32)).astype(BF16)
    acc_copy.wait_recv()
    total = acc[pl.ds(0, units), :] + acc_in[...]
    gd_ref[...] = jnp.where(lax.rem(d, 2) == 1, total[:, 64:512], total[:, 0:448]).astype(BF16)

    for sent in (tab_copy, tok_copy, hid_copy, w_copy, mix_copy, gh_copy, acc_copy, ag_leap, rs_leap):
        sent.wait_send()
    each(1, reach + 1, lambda i: tab(i, 0).wait_send())
    each(1, reach + 1, lambda i: tab(i, reach).wait_send())
    each(0, leap - 1, lambda s: ag(s).wait_send())
    each(leap, last, lambda s: ag(s).wait_send())
    each(1, leap, lambda s: rs(s).wait_send())
    each(leap + 1, half, lambda s: rs(s).wait_send())

    @pl.when(first)
    def _():
        ag(last).wait_send()
        rs(half).wait_send()

    each(1, nd, lambda i: hw_copy(i, False).wait_send())
    each(1, nd, lambda i: block_copy(i, False).wait_send())


def body(hidden, expert_ids, route_weight, cotangent, w_down):
    width = cotangent.shape[1]
    units = hidden.shape[1]
    nd, ne = lax.axis_size("dp"), lax.axis_size("expert")
    half, tiles = ne // 4, width // 128
    leap = 5 * half // 8
    toks = 4 * half
    vmem = pl.BlockSpec(memory_space=pltpu.VMEM)
    anywhere = pl.BlockSpec(memory_space=pl.ANY)
    dma = lambda n: pltpu.SemaphoreType.DMA((n,))
    mixed, grad_hidden, grad_down = pl.pallas_call(
        functools.partial(kernel, nd, ne, leap),
        out_shape=(jax.ShapeDtypeStruct((2 * tiles, 128), BF16), jax.ShapeDtypeStruct((2 * ne, units), BF16),
                   jax.ShapeDtypeStruct((units, 448), BF16)),
        in_specs=[anywhere] * 5,
        out_specs=(vmem, vmem, vmem),
        scratch_shapes=[
            pltpu.VMEM((2, units, width), BF16),
            pltpu.VMEM(expert_ids.shape, jnp.int32),
            pltpu.VMEM(route_weight.shape, F32),
            pltpu.VMEM(cotangent.shape, BF16),
            pltpu.VMEM((8 * nd, 128), F32),
            pltpu.VMEM((8 * nd, 128), F32),
            pltpu.VMEM((2 * ne, units), BF16),
            pltpu.VMEM((2 * ne, units), BF16),
            pltpu.VMEM((2, 128), F32),
            pltpu.VMEM((2, 128), F32),
            pltpu.VMEM((half + 1, 4, 128), F32),
            pltpu.VMEM((toks, 128), F32),
            pltpu.VMEM((half + 1, 16 * nd, 128), BF16),
            pltpu.VMEM((toks * tiles, 128), F32),
            pltpu.VMEM((half, 4 * tiles, 128), BF16),
            pltpu.VMEM((half + 1, 4 * tiles, 128), BF16),
            pltpu.VMEM((4 * tiles, 128), F32),
            pltpu.VMEM((2 * tiles, 128), F32),
            pltpu.VMEM((nd, units, 2 * toks), BF16),
            pltpu.VMEM((nd, 2 * units, 16 * half), BF16),
            pltpu.VMEM((nd, half, 16, 128), BF16),
            pltpu.VMEM((16 * half, 2 * units), F32),
            pltpu.VMEM((2 * ne, units), BF16),
            pltpu.VMEM((2 * ne, units), BF16),
            pltpu.VMEM((2 * units, 512), F32),
            pltpu.VMEM((units, 512), F32),
            dma(6), dma(7), dma(7), dma(half + 1), dma(half + 1), dma(half), dma(half + 1), dma(half + 1), dma(half),
            dma(nd), dma(nd), dma(nd), dma(nd),
        ],
        compiler_params=pltpu.CompilerParams(collective_id=0, has_side_effects=True,
                                             vmem_limit_bytes=56 * 1024 * 1024),
        cost_estimate=pl.CostEstimate(flops=12 * ne * units * width, bytes_accessed=2 * units * width,
                                      transcendentals=0),
    )(expert_ids, route_weight, cotangent, hidden, w_down)
    return (mixed.reshape(2, width), grad_hidden, grad_down)


def solution(mesh):
    return jax.shard_map(
        body,
        mesh=mesh,
        in_specs=(
            P("dp", "expert"),
            P(("dp", "expert"), None),
            P(("dp", "expert"), None),
            P(("dp", "expert"), None),
            P("expert", None),
        ),
        out_specs=(P(("dp", "expert"), None), P("dp", "expert"), P("expert", "dp")),
        check_vma=False,
    )
```

```python
import functools

import jax
import jax.numpy as jnp
from jax import lax
from jax.experimental import pallas as pl
from jax.experimental.pallas import tpu as pltpu
from jax.sharding import PartitionSpec as P

MESH = pl.DeviceIdType.MESH
F32, BF16 = jnp.float32, jnp.bfloat16
NT = (((1,), (1,)), ((), ()))
TN = (((0,), (0,)), ((), ()))
LAG = 4


def onehot(rows, columns, dtype):
    return (rows == columns).astype(F32).astype(dtype)


def kernel(nd, ne, leap, back_leap, cuts, back_cuts, ids_ref, weight_ref, cot_ref, hid_ref, w_ref, mixed_ref, gh_ref, gd_ref,
           w2, ids, weights, cot, own_half, sib_half, own_hid, sib_hid, own_tab, sib_tab, table, flat, ring,
           y_buf, rs_in, rs_out, fin, mix_in, hw_t, lefts, blocks, g_acc, gh_send, gh_in, acc, acc_in,
           local_sem, sib_s, sib_r, tab_s, tab_r, ag_s, ag_r, rs_s, rs_r, hw_s, hw_r, bl_s, bl_r):
    nz, half = ne // 2, ne // 4
    toks = 4 * half
    reach = half // 2
    units = hid_ref.shape[1]
    tiles = w2.shape[2] // 128
    d, p = lax.axis_index("dp"), lax.axis_index("expert")
    z, c = p // 2, lax.rem(p, 2)
    way = 1 - 2 * c
    expert = p // 4
    base = 1 - c
    sibling = (d, p + 1 - 2 * c)

    def chip(steps):
        return (d, lax.rem(z + way * steps + 2 * nz, nz) * 2 + c)

    def copy(src, dst, send, recv, to):
        return pltpu.make_async_remote_copy(src_ref=src, dst_ref=dst, send_sem=send, recv_sem=recv,
                                            device_id=to, device_id_type=MESH)

    def each(low, high, step):
        def run(i, _):
            step(i)
            return 0
        lax.fori_loop(low, high, run, 0)

    loads = [pltpu.make_async_copy(a, b, local_sem.at[i]) for i, (a, b) in enumerate(
        ((ids_ref, ids), (weight_ref, weights), (cot_ref, cot), (hid_ref, own_hid), (w_ref, w2.at[0])))]
    for load in loads:
        load.start()

    barrier = pltpu.get_barrier_semaphore()

    def greet(to):
        pl.semaphore_signal(barrier, inc=1, device_id=to, device_id_type=MESH)

    greet(sibling)
    each(1, reach + 1, lambda i: greet(chip(-i)))
    greet(chip(-leap))
    greet(chip(1))
    greet(chip(back_leap))
    each(1, nd, lambda i: greet((lax.rem(d + i, nd), p)))

    loads[0].wait()
    loads[1].wait()
    lane = lax.broadcasted_iota(jnp.int32, (1, 128), 1)
    named = [jnp.zeros((1, 128), F32), jnp.zeros((1, 128), F32)]
    weight = [jnp.zeros((1, 128), F32), jnp.zeros((1, 128), F32)]
    for k in range(ids.shape[1]):
        for t in range(2):
            hit = ids[t:t + 1, k:k + 1] == (lane & 31)
            named[t] = jnp.where(hit, 1.0, named[t])
            weight[t] = jnp.where(hit, weights[t:t + 1, k:k + 1], weight[t])
    part = lane >> 5
    moved = jnp.where(named[0] > 0, 0.0, weight[1])
    kept = jnp.where(named[0] > 0, weight[1], 0.0)
    zero = jnp.zeros_like(moved)
    own_tab[0:1, :] = jnp.where(part == 0, weight[0], jnp.where(part == 2, moved, zero))
    own_tab[1:2, :] = jnp.where(part == 0, kept, jnp.where(part == 1, moved, zero))
    pl.semaphore_wait(barrier, 4 + reach + nd - 1)

    tab_copy = copy(own_tab, sib_tab, sib_s.at[6], sib_r.at[6], sibling)
    tok_copy = copy(own_half, sib_half, sib_s.at[0], sib_r.at[0], sibling)
    hid_copy = copy(own_hid, sib_hid, sib_s.at[1], sib_r.at[1], sibling)
    w_copy = copy(w_ref, w2.at[1], sib_s.at[2], sib_r.at[2], sibling)
    tab_copy.start()
    loads[2].wait()
    for block in range(nd):
        for q in range(4):
            tile = (block // 2) * 7 + 3 * (block % 2) + q
            own_half[pl.ds(8 * block + q, 2, stride=4), :] = cot[:, 128 * tile:128 * tile + 128].astype(F32)
    tok_copy.start()

    def tab(r, first):
        slot = first + r
        return copy(table.at[first], table.at[slot], tab_s.at[slot], tab_r.at[slot], chip(r))

    def ag_copy(source, target, h, send, steps):
        rows = pl.ds(h * (16 * nd // cuts), 16 * nd // cuts)
        return copy(ring.at[source, rows], ring.at[target, rows], ag_s.at[send * cuts + h], ag_r.at[target * cuts + h],
                    chip(steps))

    def ag(s, h):
        return ag_copy(s, s + 1, h, s, 1)

    def ag_leap(h):
        return ag_copy(0, leap, h, leap - 1, leap)

    def ag_landed(s, h):
        ag_copy(0, s, h, 0, 1).wait_recv()

    def near_step(s):
        for h in range(cuts):
            ag_landed(s, h)
            ag(s, h).start()

    def far_step(s):
        for h in range(cuts):
            ag_landed(s, h)
            if s == half - 1:
                pl.when(c == 0)(ag(s, h).start)
            else:
                ag(s, h).start()

    def rounds(low, high):
        for s in range(low, high):
            if s < leap - 1:
                near_step(s)
            far = leap + s - late
            if leap <= far < half:
                far_step(far)

    tab_copy.wait_recv()
    mine, theirs = own_tab[...], sib_tab[...]
    first = c == 0
    table[0] = jnp.concatenate([jnp.where(first, mine, theirs), jnp.where(first, theirs, mine)], axis=0)
    each(0, reach, lambda i: tab(reach - i, 0).start())
    loads[3].wait()
    hid_copy.start()
    tok_copy.wait_recv()
    mine, theirs = own_half[...].reshape(nd, 8, 128), sib_half[...].reshape(nd, 8, 128)
    ring[0] = jnp.concatenate([jnp.where(first, mine, theirs), jnp.where(first, theirs, mine)],
                              axis=1).reshape(16 * nd, 128).astype(BF16)
    late = max(1, 2 * leap - 1 - half)
    for h in range(cuts):
        ag(0, h).start()
    for h in range(cuts):
        ag_leap(h).start()
    w_copy.start()
    top = max(leap - 1, half - leap + late)
    rounds(1, min(2, top))
    tab(reach, 0).wait_recv()
    each(0, reach, lambda i: tab(reach - i, reach).start())
    rounds(2, min(4, top))
    each(1, reach, lambda i: tab(i, 0).wait_recv())
    each(1, reach + 1, lambda i: tab(i, reach).wait_recv())
    hid_copy.wait_recv()

    for i in range(half):
        flat[4 * i:4 * i + 4, :] = table[base + i]
    row = lax.broadcasted_iota(jnp.int32, (toks, 4 * nz), 0)
    column = lax.broadcasted_iota(jnp.int32, (toks, 4 * nz), 1)

    def place_of(token):
        at = z - way * ((token >> 2) + base)
        at = jnp.where(at < 0, at + nz, at)
        at = jnp.where(at >= nz, at - nz, at)
        return at * 4 + (token & 3)

    place = place_of(row)
    picked = flat[...]
    lanes = lax.broadcasted_iota(jnp.int32, (toks, 128), 1)

    def coefficient(k):
        return jnp.sum(jnp.where(lanes == expert + 32 * k, picked, 0.0), axis=1, keepdims=True)

    keep, shift, give = coefficient(0), coefficient(1), coefficient(2)
    both = jnp.concatenate([own_hid[...], sib_hid[...]], axis=1)
    at = jnp.dot(onehot(place, column, BF16), both, preferred_element_type=F32)
    before = jnp.dot(onehot(place - 1, column, BF16), both, preferred_element_type=F32)
    hw = (keep * at + shift * before).astype(BF16)

    loads[4].wait()
    w_copy.wait_recv()

    def forward(m):
        at_column = pl.multiple_of(m * 896, 128)
        columns = w2[:, :, pl.ds(at_column, 896)].reshape(2 * units, 896)
        part = jnp.dot(hw, columns, preferred_element_type=F32)
        for k in range(7):
            y_buf[pl.ds(m * 7 + k, toks, stride=tiles), :] = part[:, 128 * k:128 * k + 128]

    each(0, nd // 2, forward)

    piece = 4 * tiles // back_cuts

    def y_at(s, h):
        return y_buf[pl.ds(pl.multiple_of((s - base) * 4 * tiles + h * piece, 8), piece), :]

    def rs_copy(source, target, h, steps):
        rows = pl.ds(h * piece, piece)
        return copy(rs_out.at[source, rows], rs_in.at[target, rows], rs_s.at[source * back_cuts + h],
                    rs_r.at[target * back_cuts + h], chip(-steps))

    def rs(s, h):
        return rs_copy(s, s - 1, h, 1)

    def rs_send(s, h):
        if s == back_leap:
            rs_copy(s, s - 1, h, s).start()
        else:
            rs(s, h).start()

    def rs_landed(s, h):
        rs_copy(1, s, h, 1).wait_recv()

    def rs_begin(s, h):
        rs_out[s, pl.ds(h * piece, piece), :] = y_at(s, h).astype(BF16)

    def rs_add(s, h):
        rs_landed(s, h)
        rs_out[s, pl.ds(h * piece, piece), :] = (
            y_at(s, h) + rs_in[s, pl.ds(h * piece, piece), :].astype(F32)).astype(BF16)

    last = half - 1

    @pl.when(first)
    def _():
        for h in range(back_cuts):
            rs_begin(half, h)
            rs_send(half, h)

    for h in range(back_cuts):
        rs_begin(back_leap - 1, h)
        rs_send(back_leap - 1, h)
    rounds(4, min(6, top))

    spot_row = lax.broadcasted_iota(jnp.int32, (toks, 2 * toks), 0)
    spot_column = lax.broadcasted_iota(jnp.int32, (toks, 2 * toks), 1)
    turned = lax.dot_general(hw[:, :units], onehot(spot_row, spot_column, BF16), TN, preferred_element_type=F32)
    turned = turned + lax.dot_general(hw[:, units:], onehot(spot_row + toks, spot_column, BF16), TN,
                                      preferred_element_type=F32)
    hw_t[d] = turned.astype(BF16)

    def hw_copy(i, back):
        slot = lax.rem(d + nd - i, nd) if back else d
        return copy(hw_t.at[d], hw_t.at[slot], hw_s.at[i], hw_r.at[i], (lax.rem(d + i, nd), p))

    each(1, nd, lambda i: hw_copy(i, False).start())

    for h in range(back_cuts):
        pl.when(first)(functools.partial(rs_add, last, h))
        pl.when(c == 1)(functools.partial(rs_begin, last, h))
        rs_send(last, h)

    far_left = list(range(last - 1, back_leap - 1, -1))
    near_left = list(range(back_leap - 2, 0, -1))
    order = []
    while far_left or near_left:
        if near_left:
            order.append(near_left.pop(0))
        if far_left:
            order.append(far_left.pop(0))

    def block_copy(i, back):
        to = lax.rem(d + i, nd)
        slot = lax.rem(d + nd - i, nd) if back else d
        return copy(ring.at[pl.ds(base, half), pl.ds(pl.multiple_of(16 * to, 16), 16), :], blocks.at[slot],
                    bl_s.at[i], bl_r.at[i], (to, p))

    own_block = pltpu.make_async_copy(
        ring.at[pl.ds(base, half), pl.ds(pl.multiple_of(16 * d, 16), 16), :], blocks.at[d], local_sem.at[5])
    quarter = lax.broadcasted_iota(jnp.int32, (16 * half, 128), 0) & 3

    def spread(values, low):
        return [jnp.where(quarter == k, values, jnp.zeros_like(values)) for k in range(low, 4)]

    g_acc[...] = jnp.zeros_like(g_acc)

    def backward(m):
        at_column = pl.multiple_of(m * 896, 128)
        columns = w2[:, :, pl.ds(at_column, 896)].reshape(2 * units, 896)
        even = ring[pl.ds(base, half), pl.ds(pl.multiple_of(32 * m, 16), 16), :].reshape(16 * half, 128)
        odd = ring[pl.ds(base, half), pl.ds(pl.multiple_of(32 * m + 16, 16), 16), :].reshape(16 * half, 128)
        wide = jnp.concatenate(spread(even, 0) + spread(odd, 1), axis=1)
        g_acc[...] += lax.dot_general(wide, columns, NT, preferred_element_type=F32)

    repeat_row = lax.broadcasted_iota(jnp.int32, (2 * toks, 16 * half), 0)
    repeat_column = lax.broadcasted_iota(jnp.int32, (2 * toks, 16 * half), 1) >> 2
    repeat_own = onehot(repeat_row, repeat_column, BF16)
    repeat_sib = onehot(repeat_row, repeat_column + toks, BF16)

    def make_left(slot):
        lefts[slot] = jnp.concatenate([
            jnp.dot(hw_t[slot], repeat_own, preferred_element_type=F32),
            jnp.dot(hw_t[slot], repeat_sib, preferred_element_type=F32)], axis=0).astype(BF16)

    def peer_left(i):
        hw_copy(i, True).wait_recv()
        make_left(lax.rem(d + nd - i, nd))

    begun = 0
    going = 6
    gathered = False
    for count, s in enumerate(order):
        for h in range(back_cuts):
            rs_add(s, h)
            rs_send(s, h)
        if count % 2 == 1 or count == len(order) - 1:
            if going < top:
                rounds(going, going + 1)
                going += 1
            elif not gathered:
                gathered = True

                for h in range(cuts):
                    pl.when(first)(functools.partial(ag_landed, half, h))
                    ag_landed(leap - 1, h)
                each(1, nd, lambda i: block_copy(i, False).start())
                own_block.start()
        if gathered and begun < nd // 2:
            stop = min(begun + max(1, nd // 8), nd // 2)
            each(begun, stop, backward)
            begun = stop
        if count == len(order) - 2:
            make_left(d)
            each(1, nd // 2, peer_left)
        if count == len(order) - 1:
            if len(order) < 2:
                make_left(d)
                each(1, nd // 2, peer_left)
            each(nd // 2, nd, peer_left)
    assert gathered
    each(begun, nd // 2, backward)

    fours = onehot(lax.broadcasted_iota(jnp.int32, (toks, 16 * half), 0),
                   lax.broadcasted_iota(jnp.int32, (toks, 16 * half), 1) >> 2, F32)
    back = jnp.dot(fours, g_acc[...], preferred_element_type=F32, precision=lax.Precision.HIGHEST)
    slots = (keep * back + give * pltpu.roll(back, toks - 1, 0)).astype(BF16)
    home = place_of(lax.broadcasted_iota(jnp.int32, (4 * nz, toks), 1))
    home_row = lax.broadcasted_iota(jnp.int32, (4 * nz, toks), 0)
    placed = jnp.dot(onehot(home, home_row, BF16), slots, preferred_element_type=F32).astype(BF16)
    gh_send[...] = placed[:, units:]
    gh_copy = copy(gh_send, gh_in, sib_s.at[4], sib_r.at[4], sibling)
    gh_copy.start()

    def add_block(slot):
        wide = jnp.concatenate(spread(blocks[slot].reshape(16 * half, 128), 0), axis=1)
        return jnp.dot(lefts[slot], wide, preferred_element_type=F32)

    own_block.wait()
    acc[...] = add_block(d)

    def peer(i):
        block_copy(i, True).wait_recv()
        acc[...] += add_block(lax.rem(d + nd - i, nd))

    each(1, nd, peer)
    acc_copy = copy(acc.at[pl.ds(units, units)], acc_in, sib_s.at[5], sib_r.at[5], sibling)
    acc_copy.start()

    for h in range(back_cuts):
        rs_landed(back_leap - 1, h)
    for h in range(back_cuts):
        rs_landed(0, h)
    arrived = rs_in[0].astype(F32) + rs_in[back_leap - 1].astype(F32)

    @pl.when(first)
    def _():
        fin[...] = arrived

    @pl.when(c == 1)
    def _():
        fin[...] = arrived + y_buf[pl.ds(0, 4 * tiles), :]

    mix_copy = copy(fin.at[pl.ds(pl.multiple_of(2 * tiles * (1 - c), 8), 2 * tiles)], mix_in,
                    sib_s.at[3], sib_r.at[3], sibling)
    mix_copy.start()

    mix_copy.wait_recv()
    own_rows = fin[pl.ds(pl.multiple_of(2 * tiles * c, 8), 2 * tiles), :]
    mixed_ref[...] = (own_rows + mix_in[...]).astype(BF16)
    gh_copy.wait_recv()
    gh_ref[...] = (placed[:, :units].astype(F32) + gh_in[...].astype(F32)).astype(BF16)
    acc_copy.wait_recv()
    total = acc[pl.ds(0, units), :] + acc_in[...]
    gd_ref[...] = jnp.where(lax.rem(d, 2) == 1, total[:, 64:512], total[:, 0:448]).astype(BF16)

    for sent in (tab_copy, tok_copy, hid_copy, w_copy, mix_copy, gh_copy, acc_copy):
        sent.wait_send()
    each(1, reach + 1, lambda i: tab(i, 0).wait_send())
    each(1, reach + 1, lambda i: tab(i, reach).wait_send())
    for h in range(cuts):
        ag_leap(h).wait_send()
        each(0, leap - 1, lambda s: ag(s, h).wait_send())
        each(leap, last, lambda s: ag(s, h).wait_send())
        pl.when(first)(ag(last, h).wait_send)
    for h in range(back_cuts):
        each(1, half, lambda s: rs(s, h).wait_send())
        pl.when(first)(rs(half, h).wait_send)
    each(1, nd, lambda i: hw_copy(i, False).wait_send())
    each(1, nd, lambda i: block_copy(i, False).wait_send())


def body(hidden, expert_ids, route_weight, cotangent, w_down):
    width = cotangent.shape[1]
    units = hidden.shape[1]
    nd, ne = lax.axis_size("dp"), lax.axis_size("expert")
    half, tiles = ne // 4, width // 128
    leap = 5 * half // 8
    back_leap, cuts, back_cuts = leap - half // 16, 2, 1
    toks = 4 * half
    vmem = pl.BlockSpec(memory_space=pltpu.VMEM)
    anywhere = pl.BlockSpec(memory_space=pl.ANY)
    dma = lambda n: pltpu.SemaphoreType.DMA((n,))
    mixed, grad_hidden, grad_down = pl.pallas_call(
        functools.partial(kernel, nd, ne, leap, back_leap, cuts, back_cuts),
        out_shape=(jax.ShapeDtypeStruct((2 * tiles, 128), BF16), jax.ShapeDtypeStruct((2 * ne, units), BF16),
                   jax.ShapeDtypeStruct((units, 448), BF16)),
        in_specs=[anywhere] * 5,
        out_specs=(vmem, vmem, vmem),
        scratch_shapes=[
            pltpu.VMEM((2, units, width), BF16),
            pltpu.VMEM(expert_ids.shape, jnp.int32),
            pltpu.VMEM(route_weight.shape, F32),
            pltpu.VMEM(cotangent.shape, BF16),
            pltpu.VMEM((8 * nd, 128), F32),
            pltpu.VMEM((8 * nd, 128), F32),
            pltpu.VMEM((2 * ne, units), BF16),
            pltpu.VMEM((2 * ne, units), BF16),
            pltpu.VMEM((2, 128), F32),
            pltpu.VMEM((2, 128), F32),
            pltpu.VMEM((half + 1, 4, 128), F32),
            pltpu.VMEM((toks, 128), F32),
            pltpu.VMEM((half + 1, 16 * nd, 128), BF16),
            pltpu.VMEM((toks * tiles, 128), F32),
            pltpu.VMEM((half, 4 * tiles, 128), BF16),
            pltpu.VMEM((half + 1, 4 * tiles, 128), BF16),
            pltpu.VMEM((4 * tiles, 128), F32),
            pltpu.VMEM((2 * tiles, 128), F32),
            pltpu.VMEM((nd, units, 2 * toks), BF16),
            pltpu.VMEM((nd, 2 * units, 16 * half), BF16),
            pltpu.VMEM((nd, half, 16, 128), BF16),
            pltpu.VMEM((16 * half, 2 * units), F32),
            pltpu.VMEM((2 * ne, units), BF16),
            pltpu.VMEM((2 * ne, units), BF16),
            pltpu.VMEM((2 * units, 512), F32),
            pltpu.VMEM((units, 512), F32),
            dma(6), dma(7), dma(7), dma(half + 1), dma(half + 1), dma(cuts * half), dma(cuts * (half + 1)), dma(back_cuts * (half + 1)), dma(back_cuts * half),
            dma(nd), dma(nd), dma(nd), dma(nd),
        ],
        compiler_params=pltpu.CompilerParams(collective_id=0, has_side_effects=True,
                                             vmem_limit_bytes=56 * 1024 * 1024),
        cost_estimate=pl.CostEstimate(flops=12 * ne * units * width, bytes_accessed=2 * units * width,
                                      transcendentals=0),
    )(expert_ids, route_weight, cotangent, hidden, w_down)
    return (mixed.reshape(2, width), grad_hidden, grad_down)


def solution(mesh):
    return jax.shard_map(
        body,
        mesh=mesh,
        in_specs=(
            P("dp", "expert"),
            P(("dp", "expert"), None),
            P(("dp", "expert"), None),
            P(("dp", "expert"), None),
            P("expert", None),
        ),
        out_specs=(P(("dp", "expert"), None), P("dp", "expert"), P("expert", "dp")),
        check_vma=False,
    )
```

```python
import functools

import jax
import jax.numpy as jnp
from jax import lax
from jax.experimental import pallas as pl
from jax.experimental.pallas import tpu as pltpu
from jax.sharding import PartitionSpec as P

MESH = pl.DeviceIdType.MESH
F32, BF16 = jnp.float32, jnp.bfloat16
NT = (((1,), (1,)), ((), ()))
TN = (((0,), (0,)), ((), ()))
LAG = 4


def onehot(rows, columns, dtype):
    return (rows == columns).astype(F32).astype(dtype)


def kernel(nd, ne, leap, back_leap, cuts, back_cuts, ids_ref, weight_ref, cot_ref, hid_ref, w_ref, mixed_ref, gh_ref, gd_ref,
           w2, ids, weights, cot, own_half, sib_half, own_hid, sib_hid, own_tab, sib_tab, table, flat, ring,
           y_buf, rs_in, rs_out, fin, mix_in, hw_t, lefts, blocks, g_acc, gh_send, gh_in, acc, acc_in,
           local_sem, sib_s, sib_r, tab_s, tab_r, ag_s, ag_r, rs_s, rs_r, hw_s, hw_r, bl_s, bl_r):
    nz, half = ne // 2, ne // 4
    toks = 4 * half
    reach = half // 2
    units = hid_ref.shape[1]
    tiles = w2.shape[2] // 128
    d, p = lax.axis_index("dp"), lax.axis_index("expert")
    z, c = p // 2, lax.rem(p, 2)
    way = 1 - 2 * c
    expert = p // 4
    base = 1 - c
    sibling = (d, p + 1 - 2 * c)

    def chip(steps):
        return (d, lax.rem(z + way * steps + 2 * nz, nz) * 2 + c)

    def copy(src, dst, send, recv, to):
        return pltpu.make_async_remote_copy(src_ref=src, dst_ref=dst, send_sem=send, recv_sem=recv,
                                            device_id=to, device_id_type=MESH)

    def each(low, high, step):
        def run(i, _):
            step(i)
            return 0
        lax.fori_loop(low, high, run, 0)

    loads = [pltpu.make_async_copy(a, b, local_sem.at[i]) for i, (a, b) in enumerate(
        ((ids_ref, ids), (weight_ref, weights), (cot_ref, cot), (hid_ref, own_hid), (w_ref, w2.at[0])))]
    for load in loads:
        load.start()

    barrier = pltpu.get_barrier_semaphore()

    def greet(to):
        pl.semaphore_signal(barrier, inc=1, device_id=to, device_id_type=MESH)

    greet(sibling)
    each(1, reach + 1, lambda i: greet(chip(-i)))
    greet(chip(-leap))
    greet(chip(1))
    greet(chip(back_leap))
    each(1, nd, lambda i: greet((lax.rem(d + i, nd), p)))

    loads[0].wait()
    loads[1].wait()
    lane = lax.broadcasted_iota(jnp.int32, (1, 128), 1)
    named = [jnp.zeros((1, 128), F32), jnp.zeros((1, 128), F32)]
    weight = [jnp.zeros((1, 128), F32), jnp.zeros((1, 128), F32)]
    for k in range(ids.shape[1]):
        for t in range(2):
            hit = ids[t:t + 1, k:k + 1] == (lane & 31)
            named[t] = jnp.where(hit, 1.0, named[t])
            weight[t] = jnp.where(hit, weights[t:t + 1, k:k + 1], weight[t])
    part = lane >> 5
    moved = jnp.where(named[0] > 0, 0.0, weight[1])
    kept = jnp.where(named[0] > 0, weight[1], 0.0)
    zero = jnp.zeros_like(moved)
    own_tab[0:1, :] = jnp.where(part == 0, weight[0], jnp.where(part == 2, moved, zero))
    own_tab[1:2, :] = jnp.where(part == 0, kept, jnp.where(part == 1, moved, zero))
    pl.semaphore_wait(barrier, 4 + reach + nd - 1)

    tab_copy = copy(own_tab, sib_tab, sib_s.at[6], sib_r.at[6], sibling)
    tok_copy = copy(own_half, sib_half, sib_s.at[0], sib_r.at[0], sibling)
    hid_copy = copy(own_hid, sib_hid, sib_s.at[1], sib_r.at[1], sibling)
    w_copy = copy(w_ref, w2.at[1], sib_s.at[2], sib_r.at[2], sibling)
    tab_copy.start()
    loads[2].wait()
    for block in range(nd):
        for q in range(4):
            tile = (block // 2) * 7 + 3 * (block % 2) + q
            own_half[pl.ds(8 * block + q, 2, stride=4), :] = cot[:, 128 * tile:128 * tile + 128].astype(F32)
    tok_copy.start()

    def tab(r, first):
        slot = first + r
        return copy(table.at[first], table.at[slot], tab_s.at[slot], tab_r.at[slot], chip(r))

    def ag_copy(source, target, h, send, steps):
        rows = pl.ds(h * (16 * nd // cuts), 16 * nd // cuts)
        return copy(ring.at[source, rows], ring.at[target, rows], ag_s.at[send * cuts + h], ag_r.at[target * cuts + h],
                    chip(steps))

    def ag(s, h):
        return ag_copy(s, s + 1, h, s, 1)

    def ag_leap(h):
        return ag_copy(0, leap, h, leap - 1, leap)

    def ag_landed(s, h):
        ag_copy(0, s, h, 0, 1).wait_recv()

    def near_step(s):
        for h in range(cuts):
            ag_landed(s, h)
            ag(s, h).start()

    def far_step(s):
        for h in range(cuts):
            ag_landed(s, h)
            if s == half - 1:
                pl.when(c == 0)(ag(s, h).start)
            else:
                ag(s, h).start()

    def rounds(low, high):
        for s in range(low, high):
            if s < leap - 1:
                near_step(s)
            far = leap + s - late
            if leap <= far < half:
                far_step(far)

    tab_copy.wait_recv()
    mine, theirs = own_tab[...], sib_tab[...]
    first = c == 0
    table[0] = jnp.concatenate([jnp.where(first, mine, theirs), jnp.where(first, theirs, mine)], axis=0)
    each(0, reach, lambda i: tab(reach - i, 0).start())
    loads[3].wait()
    hid_copy.start()
    tok_copy.wait_recv()
    mine, theirs = own_half[...].reshape(nd, 8, 128), sib_half[...].reshape(nd, 8, 128)
    ring[0] = jnp.concatenate([jnp.where(first, mine, theirs), jnp.where(first, theirs, mine)],
                              axis=1).reshape(16 * nd, 128).astype(BF16)
    late = max(1, 2 * leap - 1 - half)
    for h in range(cuts):
        ag(0, h).start()
    for h in range(cuts):
        ag_leap(h).start()
    w_copy.start()
    top = max(leap - 1, half - leap + late)
    rounds(1, min(2, top))
    tab(reach, 0).wait_recv()
    each(0, reach, lambda i: tab(reach - i, reach).start())
    rounds(2, min(4, top))
    each(1, reach, lambda i: tab(i, 0).wait_recv())
    each(1, reach + 1, lambda i: tab(i, reach).wait_recv())
    hid_copy.wait_recv()

    for i in range(half):
        flat[4 * i:4 * i + 4, :] = table[base + i]
    row = lax.broadcasted_iota(jnp.int32, (toks, 4 * nz), 0)
    column = lax.broadcasted_iota(jnp.int32, (toks, 4 * nz), 1)

    def place_of(token):
        at = z - way * ((token >> 2) + base)
        at = jnp.where(at < 0, at + nz, at)
        at = jnp.where(at >= nz, at - nz, at)
        return at * 4 + (token & 3)

    place = place_of(row)
    picked = flat[...]
    lanes = lax.broadcasted_iota(jnp.int32, (toks, 128), 1)

    def coefficient(k):
        return jnp.sum(jnp.where(lanes == expert + 32 * k, picked, 0.0), axis=1, keepdims=True)

    keep, shift, give = coefficient(0), coefficient(1), coefficient(2)
    both = jnp.concatenate([own_hid[...], sib_hid[...]], axis=1)
    at = jnp.dot(onehot(place, column, BF16), both, preferred_element_type=F32)
    before = jnp.dot(onehot(place - 1, column, BF16), both, preferred_element_type=F32)
    hw = (keep * at + shift * before).astype(BF16)

    loads[4].wait()
    w_copy.wait_recv()

    def forward(m):
        at_column = pl.multiple_of(m * 896, 128)
        columns = w2[:, :, pl.ds(at_column, 896)].reshape(2 * units, 896)
        part = jnp.dot(hw, columns, preferred_element_type=F32)
        for k in range(7):
            y_buf[pl.ds(m * 7 + k, toks, stride=tiles), :] = part[:, 128 * k:128 * k + 128]

    each(0, nd // 2, forward)

    piece = 4 * tiles // back_cuts

    def y_at(s, h):
        return y_buf[pl.ds(pl.multiple_of((s - base) * 4 * tiles + h * piece, 8), piece), :]

    def rs_copy(source, target, h, steps):
        rows = pl.ds(h * piece, piece)
        return copy(rs_out.at[source, rows], rs_in.at[target, rows], rs_s.at[source * back_cuts + h],
                    rs_r.at[target * back_cuts + h], chip(-steps))

    def rs(s, h):
        return rs_copy(s, s - 1, h, 1)

    def rs_send(s, h):
        if s == back_leap:
            rs_copy(s, s - 1, h, s).start()
        else:
            rs(s, h).start()

    def rs_landed(s, h):
        rs_copy(1, s, h, 1).wait_recv()

    def rs_begin(s, h):
        rs_out[s, pl.ds(h * piece, piece), :] = y_at(s, h).astype(BF16)

    def rs_add(s, h):
        rs_landed(s, h)
        rs_out[s, pl.ds(h * piece, piece), :] = (
            y_at(s, h) + rs_in[s, pl.ds(h * piece, piece), :].astype(F32)).astype(BF16)

    last = half - 1

    @pl.when(first)
    def _():
        for h in range(back_cuts):
            rs_begin(half, h)
            rs_send(half, h)

    for h in range(back_cuts):
        rs_begin(back_leap - 1, h)
        rs_send(back_leap - 1, h)
    rounds(4, min(6, top))

    spot_row = lax.broadcasted_iota(jnp.int32, (toks, 2 * toks), 0)
    spot_column = lax.broadcasted_iota(jnp.int32, (toks, 2 * toks), 1)
    turned = lax.dot_general(hw[:, :units], onehot(spot_row, spot_column, BF16), TN, preferred_element_type=F32)
    turned = turned + lax.dot_general(hw[:, units:], onehot(spot_row + toks, spot_column, BF16), TN,
                                      preferred_element_type=F32)
    hw_t[d] = turned.astype(BF16)

    def hw_copy(i, back):
        slot = lax.rem(d + nd - i, nd) if back else d
        return copy(hw_t.at[d], hw_t.at[slot], hw_s.at[i], hw_r.at[i], (lax.rem(d + i, nd), p))

    each(1, nd, lambda i: hw_copy(i, False).start())

    for h in range(back_cuts):
        pl.when(first)(functools.partial(rs_add, last, h))
        pl.when(c == 1)(functools.partial(rs_begin, last, h))
        rs_send(last, h)

    far_left = list(range(last - 1, back_leap - 1, -1))
    near_left = list(range(back_leap - 2, 0, -1))
    order = []
    while far_left or near_left:
        if near_left:
            order.append(near_left.pop(0))
        if far_left:
            order.append(far_left.pop(0))

    def block_copy(i, back):
        to = lax.rem(d + i, nd)
        slot = lax.rem(d + nd - i, nd) if back else d
        return copy(ring.at[pl.ds(base, half), pl.ds(pl.multiple_of(16 * to, 16), 16), :], blocks.at[slot],
                    bl_s.at[i], bl_r.at[i], (to, p))

    own_block = pltpu.make_async_copy(
        ring.at[pl.ds(base, half), pl.ds(pl.multiple_of(16 * d, 16), 16), :], blocks.at[d], local_sem.at[5])
    quarter = lax.broadcasted_iota(jnp.int32, (16 * half, 128), 0) & 3

    def spread(values, low):
        return [jnp.where(quarter == k, values, jnp.zeros_like(values)) for k in range(low, 4)]

    g_acc[...] = jnp.zeros_like(g_acc)

    def backward(m):
        at_column = pl.multiple_of(m * 896, 128)
        columns = w2[:, :, pl.ds(at_column, 896)].reshape(2 * units, 896)
        even = ring[pl.ds(base, half), pl.ds(pl.multiple_of(32 * m, 16), 16), :].reshape(16 * half, 128)
        odd = ring[pl.ds(base, half), pl.ds(pl.multiple_of(32 * m + 16, 16), 16), :].reshape(16 * half, 128)
        wide = jnp.concatenate(spread(even, 0) + spread(odd, 1), axis=1)
        g_acc[...] += lax.dot_general(wide, columns, NT, preferred_element_type=F32)

    repeat_row = lax.broadcasted_iota(jnp.int32, (2 * toks, 16 * half), 0)
    repeat_column = lax.broadcasted_iota(jnp.int32, (2 * toks, 16 * half), 1) >> 2
    repeat_own = onehot(repeat_row, repeat_column, BF16)
    repeat_sib = onehot(repeat_row, repeat_column + toks, BF16)

    def make_left(slot):
        lefts[slot] = jnp.concatenate([
            jnp.dot(hw_t[slot], repeat_own, preferred_element_type=F32),
            jnp.dot(hw_t[slot], repeat_sib, preferred_element_type=F32)], axis=0).astype(BF16)

    def peer_left(i):
        hw_copy(i, True).wait_recv()
        make_left(lax.rem(d + nd - i, nd))

    begun = 0
    going = 6
    gathered = False
    for count, s in enumerate(order):
        for h in range(back_cuts):
            rs_add(s, h)
            rs_send(s, h)
        if count % 2 == 1 or count == len(order) - 1:
            if going < top:
                rounds(going, going + 1)
                going += 1
            elif not gathered:
                gathered = True

                for h in range(cuts):
                    pl.when(first)(functools.partial(ag_landed, half, h))
                    ag_landed(leap - 1, h)
                each(1, nd, lambda i: block_copy(i, False).start())
                own_block.start()
        if gathered and begun < nd // 2:
            stop = min(begun + max(1, nd // 8), nd // 2)
            each(begun, stop, backward)
            begun = stop
        if count == len(order) - 2:
            make_left(d)
            each(1, nd // 2, peer_left)
        if count == len(order) - 1:
            if len(order) < 2:
                make_left(d)
                each(1, nd // 2, peer_left)
            each(nd // 2, nd, peer_left)
    assert gathered
    each(begun, nd // 2, backward)

    fours = onehot(lax.broadcasted_iota(jnp.int32, (toks, 16 * half), 0),
                   lax.broadcasted_iota(jnp.int32, (toks, 16 * half), 1) >> 2, F32)
    back = jnp.dot(fours, g_acc[...], preferred_element_type=F32, precision=lax.Precision.HIGHEST)
    slots = (keep * back + give * pltpu.roll(back, toks - 1, 0)).astype(BF16)
    home = place_of(lax.broadcasted_iota(jnp.int32, (4 * nz, toks), 1))
    home_row = lax.broadcasted_iota(jnp.int32, (4 * nz, toks), 0)
    placed = jnp.dot(onehot(home, home_row, BF16), slots, preferred_element_type=F32).astype(BF16)
    gh_send[...] = placed[:, units:]
    gh_copy = copy(gh_send, gh_in, sib_s.at[4], sib_r.at[4], sibling)
    gh_copy.start()

    def add_block(slot):
        wide = jnp.concatenate(spread(blocks[slot].reshape(16 * half, 128), 0), axis=1)
        return jnp.dot(lefts[slot], wide, preferred_element_type=F32)

    own_block.wait()
    acc[...] = add_block(d)

    def peer(i):
        block_copy(i, True).wait_recv()
        acc[...] += add_block(lax.rem(d + nd - i, nd))

    each(1, nd, peer)
    acc_copy = copy(acc.at[pl.ds(units, units)], acc_in, sib_s.at[5], sib_r.at[5], sibling)
    acc_copy.start()

    for h in range(back_cuts):
        rs_landed(back_leap - 1, h)
    for h in range(back_cuts):
        rs_landed(0, h)
    arrived = rs_in[0].astype(F32) + rs_in[back_leap - 1].astype(F32)

    @pl.when(first)
    def _():
        fin[...] = arrived

    @pl.when(c == 1)
    def _():
        fin[...] = arrived + y_buf[pl.ds(0, 4 * tiles), :]

    mix_copy = copy(fin.at[pl.ds(pl.multiple_of(2 * tiles * (1 - c), 8), 2 * tiles)], mix_in,
                    sib_s.at[3], sib_r.at[3], sibling)
    mix_copy.start()

    mix_copy.wait_recv()
    own_rows = fin[pl.ds(pl.multiple_of(2 * tiles * c, 8), 2 * tiles), :]
    mixed_ref[...] = (own_rows + mix_in[...]).astype(BF16)
    gh_copy.wait_recv()
    gh_ref[...] = (placed[:, :units].astype(F32) + gh_in[...].astype(F32)).astype(BF16)
    acc_copy.wait_recv()
    total = acc[pl.ds(0, units), :] + acc_in[...]
    gd_ref[...] = jnp.where(lax.rem(d, 2) == 1, total[:, 64:512], total[:, 0:448]).astype(BF16)

    for sent in (tab_copy, tok_copy, hid_copy, w_copy, mix_copy, gh_copy, acc_copy):
        sent.wait_send()
    each(1, reach + 1, lambda i: tab(i, 0).wait_send())
    each(1, reach + 1, lambda i: tab(i, reach).wait_send())
    for h in range(cuts):
        ag_leap(h).wait_send()
        each(0, leap - 1, lambda s: ag(s, h).wait_send())
        each(leap, last, lambda s: ag(s, h).wait_send())
        pl.when(first)(ag(last, h).wait_send)
    for h in range(back_cuts):
        each(1, half, lambda s: rs(s, h).wait_send())
        pl.when(first)(rs(half, h).wait_send)
    each(1, nd, lambda i: hw_copy(i, False).wait_send())
    each(1, nd, lambda i: block_copy(i, False).wait_send())


def body(hidden, expert_ids, route_weight, cotangent, w_down):
    width = cotangent.shape[1]
    units = hidden.shape[1]
    nd, ne = lax.axis_size("dp"), lax.axis_size("expert")
    half, tiles = ne // 4, width // 128
    leap = 5 * half // 8
    back_leap, cuts, back_cuts = leap - half // 16, 2, 2
    toks = 4 * half
    vmem = pl.BlockSpec(memory_space=pltpu.VMEM)
    anywhere = pl.BlockSpec(memory_space=pl.ANY)
    dma = lambda n: pltpu.SemaphoreType.DMA((n,))
    mixed, grad_hidden, grad_down = pl.pallas_call(
        functools.partial(kernel, nd, ne, leap, back_leap, cuts, back_cuts),
        out_shape=(jax.ShapeDtypeStruct((2 * tiles, 128), BF16), jax.ShapeDtypeStruct((2 * ne, units), BF16),
                   jax.ShapeDtypeStruct((units, 448), BF16)),
        in_specs=[anywhere] * 5,
        out_specs=(vmem, vmem, vmem),
        scratch_shapes=[
            pltpu.VMEM((2, units, width), BF16),
            pltpu.VMEM(expert_ids.shape, jnp.int32),
            pltpu.VMEM(route_weight.shape, F32),
            pltpu.VMEM(cotangent.shape, BF16),
            pltpu.VMEM((8 * nd, 128), F32),
            pltpu.VMEM((8 * nd, 128), F32),
            pltpu.VMEM((2 * ne, units), BF16),
            pltpu.VMEM((2 * ne, units), BF16),
            pltpu.VMEM((2, 128), F32),
            pltpu.VMEM((2, 128), F32),
            pltpu.VMEM((half + 1, 4, 128), F32),
            pltpu.VMEM((toks, 128), F32),
            pltpu.VMEM((half + 1, 16 * nd, 128), BF16),
            pltpu.VMEM((toks * tiles, 128), F32),
            pltpu.VMEM((half, 4 * tiles, 128), BF16),
            pltpu.VMEM((half + 1, 4 * tiles, 128), BF16),
            pltpu.VMEM((4 * tiles, 128), F32),
            pltpu.VMEM((2 * tiles, 128), F32),
            pltpu.VMEM((nd, units, 2 * toks), BF16),
            pltpu.VMEM((nd, 2 * units, 16 * half), BF16),
            pltpu.VMEM((nd, half, 16, 128), BF16),
            pltpu.VMEM((16 * half, 2 * units), F32),
            pltpu.VMEM((2 * ne, units), BF16),
            pltpu.VMEM((2 * ne, units), BF16),
            pltpu.VMEM((2 * units, 512), F32),
            pltpu.VMEM((units, 512), F32),
            dma(6), dma(7), dma(7), dma(half + 1), dma(half + 1), dma(cuts * half), dma(cuts * (half + 1)), dma(back_cuts * (half + 1)), dma(back_cuts * half),
            dma(nd), dma(nd), dma(nd), dma(nd),
        ],
        compiler_params=pltpu.CompilerParams(collective_id=0, has_side_effects=True,
                                             vmem_limit_bytes=56 * 1024 * 1024),
        cost_estimate=pl.CostEstimate(flops=12 * ne * units * width, bytes_accessed=2 * units * width,
                                      transcendentals=0),
    )(expert_ids, route_weight, cotangent, hidden, w_down)
    return (mixed.reshape(2, width), grad_hidden, grad_down)


def solution(mesh):
    return jax.shard_map(
        body,
        mesh=mesh,
        in_specs=(
            P("dp", "expert"),
            P(("dp", "expert"), None),
            P(("dp", "expert"), None),
            P(("dp", "expert"), None),
            P("expert", None),
        ),
        out_specs=(P(("dp", "expert"), None), P("dp", "expert"), P("expert", "dp")),
        check_vma=False,
    )
```
